512 devices in a mesh: feat: 64 (over z, x, core), dom: 8 (over y).
Axes of the slice: x: 4, y: 8, z: 8, core: 2. Of those that a mesh axis runs over, the one named last changes fastest.
Arguments:
- features: bfloat16 [8, 1024, 8192], P('dom', 'feat'), may hold values from -6 to 6
- weight: bfloat16 [1024, 1024], P('feat'), may hold values from -0.1875 to 0.1875
- tile_bank: bfloat16 [4, 128, 128], replicated, may hold values from -0.5 to 0.5
- neighbors: int32 [8, 64, 8], P('dom'), may hold values from 0 to 95, as said below
- tile_ids: int32 [8, 64, 8], P('dom'), may hold values from 0 to 3
- edge_weight: bfloat16 [8, 64, 8], P('dom'), may hold values from 0.099609375 to 1
- counts: int32 [8, 64], P('dom'), may hold values from 2 to 8, as said below
- boundary: int32 [8, 8, 4], P(None, 'dom'), may hold values from 0 to 63
- cotangent: bfloat16 [8, 1024, 8192], P('dom', None, 'feat'), may hold values from -16 to 16
Outputs:
- activations: bfloat16 [8, 1024, 8192], P('dom', None, 'feat')
- feature_grad: bfloat16 [8, 1024, 8192], P('dom', 'feat')
- weight_grad: float32 [1024, 1024], P('feat')
The draws below stay inside these ranges and needn't reach their ends.
Inputs may be any that keep to these rules, and one draw needn't show every extreme that they name: `neighbors`: slot 0 of block row r names r itself; slot 1 names an entry of 64 or more, and every entry from 64 to 95 is slot 1 of some row of each partition. `counts`: slots at or after a row's count are unused; each partition has a row with all 8 slots used.
All inputs are finite; a program needn't handle non-finite values.
Results may differ from the reference program's by a relative error of at most 0.015.
Values may be sent and summed in bfloat16 or wider, within the bound.
A program may use at most 64 MiB of HBM per device.

```python
import math
import jax
import jax.numpy as jnp
from jax import lax

F = 1024
TILE = 128
NBANK = 4
K = 8
VP = 8192
NBLK = 64
PARTS_SIZE = 8
BND = 4
NPOOL = 96
VERTS = 65536


def draw_counts(key, part):
    key = jax.random.fold_in(key, 11)
    key_one, key_two = jax.random.split(key)
    base_counts = jax.random.randint(key_one, (PARTS_SIZE, NBLK), 2, K + 1)
    top_rows = jax.random.randint(key_two, (PARTS_SIZE, 1), 0, NBLK)
    row_ids = jnp.arange(NBLK)[None, :]
    return jnp.where(row_ids == top_rows, K, base_counts).astype(jnp.int32)


def draw_neighbors(key, part):
    key = jax.random.fold_in(key, 23)
    key_one, key_two = jax.random.split(key)
    random_slots = jax.random.randint(key_one, (PARTS_SIZE, NBLK, K), 0, NPOOL)
    shuffled = jax.vmap(lambda inner: jax.random.permutation(inner, NBLK))(jax.random.split(key_two, PARTS_SIZE))
    second_slot = NBLK + shuffled % (PARTS_SIZE * BND)
    row_ids = jnp.broadcast_to(jnp.arange(NBLK)[None, :], (PARTS_SIZE, NBLK))
    random_slots = random_slots.at[:, :, 0].set(row_ids)
    random_slots = random_slots.at[:, :, 1].set(second_slot)
    return random_slots.astype(jnp.int32)


def with_ends(values, own_key, low, largest):
    longest = values.shape.index(max(values.shape))
    spots = []
    for shift in (0, 1):
        where = [jax.random.randint(jax.random.fold_in(own_key, axis), (), 0, length) for axis, length in enumerate(values.shape)]
        where[longest] = (where[longest] + shift) % values.shape[longest]
        spots.append(tuple(where))
    return values.at[spots[0]].set(low).at[spots[1]].set(largest)


def spiked(drawn, key, source, target, parts, factor):
    owner, partner = [(jnp.arange(drawn.shape[axis_at]) // (drawn.shape[axis_at] // parts)).reshape([-1 if axis == axis_at else 1 for axis in range(drawn.ndim)]) for axis_at in (source, target)]
    chosen = jax.random.permutation(key, parts)[partner]
    strong = (owner == chosen) | (owner == (partner + parts // 2) % parts)
    return jnp.where(strong, factor * drawn, drawn)


def levels(rng, dims, shards, low, largest):
    def one(axis_at, shards_of):
        steps = jax.random.uniform(jax.random.fold_in(jax.random.fold_in(rng, 6), axis_at), (shards_of,), jnp.float32, low / len(shards), largest / len(shards))
        return jnp.repeat(jnp.exp(steps), dims[axis_at] // shards_of).reshape((-1,) + (1,) * (len(dims) - axis_at - 1))

    loudness = one(*shards[0])
    for cut in shards[1:]:
        loudness = loudness * one(*cut)
    return loudness


def scatter_about(rng, dims, deviation, reach, shards=(), held_as=jnp.bfloat16):
    result = jax.random.normal(rng, dims, jnp.float32) * deviation
    if len(shards) > 0:
        result = levels(rng, dims, shards, -0.22, 0.18) * result
    return jnp.clip(result, min=-reach, max=reach).astype(held_as)


def bell_draw_with(key, shape, width, limit, shards, heavy, held_as=jnp.bfloat16):
    entries = width * jax.random.normal(key, shape, jnp.float32)
    if shards:
        entries = entries * levels(key, shape, shards, -0.22, 0.18)
    return jnp.clip(spiked(entries, jax.random.fold_in(key, 3), *heavy), -limit, limit).astype(held_as)


def setup_inputs(seed: int = 0) -> dict:
    keys = jax.random.split(jax.random.key(seed), 10)
    return {
        "features": scatter_about(keys[0], (PARTS_SIZE, F, VP), 1.0, 6.0, ((0, 8), (1, 64))),
        "weight": scatter_about(keys[1], (F, F), F ** -0.5, 0.1875, ((0, 64),)),
        "tile_bank": scatter_about(keys[2], (NBANK, TILE, TILE), TILE ** -0.5, 0.5),
        "neighbors": draw_neighbors(jax.random.fold_in(keys[9], 71), 0),
        "tile_ids": with_ends(jax.random.randint(keys[4], (PARTS_SIZE, NBLK, K), 0, NBANK), jax.random.fold_in(keys[4], 1), 0, NBANK - 1).astype(jnp.int32),
        "edge_weight": jnp.clip(jnp.exp(math.log(1.0) - 2.306499 * jax.random.uniform(keys[5], (PARTS_SIZE, NBLK, K), jnp.float32) ** levels(keys[5], (PARTS_SIZE, NBLK, K), ((0, 8),), -0.2, 0.2)), 0.099609375, 1.0).astype(jnp.bfloat16),
        "counts": draw_counts(jax.random.fold_in(keys[9], 71), 0),
        "boundary": with_ends(jax.random.randint(keys[7], (PARTS_SIZE, PARTS_SIZE, BND), 0, NBLK), jax.random.fold_in(keys[7], 1), 0, NBLK - 1).astype(jnp.int32),
        "cotangent": bell_draw_with(keys[8], (PARTS_SIZE, F, VP), 1.0, 16.0, ((0, 8), (2, 64)), (2, 1, 64, 4.0)),
    }


def silu_slope(pre_act):
    sigmoid_v = jax.nn.sigmoid(pre_act)
    return sigmoid_v * (1.0 + pre_act * (1.0 - sigmoid_v))

def reference(features, weight, tile_bank, neighbors, tile_ids, edge_weight, counts, boundary, cotangent):
    feat_width = features.shape[1]
    block_count = VP // TILE
    bank_wide = tile_bank.astype(jnp.float32)
    blocks = features.reshape(PARTS_SIZE, feat_width, block_count, TILE)
    selector = jnp.arange(NBANK, dtype=jnp.int32)
    slot_ids = jnp.arange(K, dtype=jnp.int32)
    activated = []
    weight_sum = jnp.zeros((F, F), jnp.float32)
    local_grads = []
    sent_grads = []
    for target in range(PARTS_SIZE):
        remote_x = [blocks[source][:, boundary[target, source], :] for source in range(PARTS_SIZE)]
        pool_x = jnp.concatenate([blocks[target]] + remote_x, axis=1)
        active = (tile_ids[target][:, :, None] == selector[None, None, :]) & (slot_ids[None, :, None] < counts[target][:, None, None])
        coeffs = jnp.where(active, edge_weight[target][:, :, None], jnp.zeros((), edge_weight.dtype)).astype(jnp.bfloat16)
        coeff_wide = coeffs.astype(jnp.float32)
        mixed_sum = jnp.zeros((block_count, NBANK, feat_width, TILE), jnp.float32)
        for slot_id in range(K):
            picked = jnp.take(pool_x, neighbors[target, :, slot_id], axis=1).astype(jnp.float32)
            mixed_sum = mixed_sum + coeff_wide[:, slot_id, :, None, None] * jnp.transpose(picked, (1, 0, 2))[:, None, :, :]
        mixed_wide = lax.optimization_barrier(mixed_sum.astype(jnp.bfloat16)).astype(jnp.float32)
        aggregated = jnp.einsum('rtfv,tuv->fru', mixed_wide, bank_wide).astype(jnp.bfloat16).reshape(feat_width, VP)
        pre_act = jnp.dot(weight, aggregated, preferred_element_type=jnp.float32)
        activated.append(jax.nn.silu(pre_act).astype(jnp.bfloat16))
        slope_bf = (cotangent[target].astype(jnp.float32) * silu_slope(pre_act)).astype(jnp.bfloat16)
        weight_sum = weight_sum + lax.dot_general(slope_bf, aggregated, (((1,), (1,)), ((), ())), preferred_element_type=jnp.float32)
        agg_grad = lax.dot_general(weight, slope_bf, (((0,), (0,)), ((), ())), preferred_element_type=jnp.float32).astype(jnp.bfloat16)
        agg_wide = lax.optimization_barrier(agg_grad).astype(jnp.float32).reshape(feat_width, block_count, TILE)
        back_mix = jnp.einsum('fru,tuv->rtfv', agg_wide, bank_wide).astype(jnp.bfloat16)
        back_wide = lax.optimization_barrier(back_mix).astype(jnp.float32)
        edge_grad = jnp.einsum('rkt,rtfv->rkfv', coeff_wide, back_wide)
        pool_grad = jax.ops.segment_sum(edge_grad.reshape(block_count * K, feat_width, TILE), neighbors[target].reshape(-1), num_segments=NPOOL)
        local_grads.append(pool_grad[:block_count])
        sent_grads.append(pool_grad[block_count:].reshape(PARTS_SIZE, BND, feat_width, TILE).astype(jnp.bfloat16))
    grads = []
    for source in range(PARTS_SIZE):
        running = local_grads[source]
        for target in range(PARTS_SIZE):
            arrived = lax.optimization_barrier(sent_grads[target][source]).astype(jnp.float32)
            running = running + jax.ops.segment_sum(arrived, boundary[target, source], num_segments=block_count)
        grads.append(jnp.transpose(running, (1, 0, 2)).reshape(feat_width, VP).astype(jnp.bfloat16))
    weight_grad = weight_sum * (1.0 / math.sqrt(VERTS))
    return (jnp.stack(activated), jnp.stack(grads), weight_grad)
```

```python
import functools
import math

import jax
import jax.numpy as jnp
from jax import lax
from jax.experimental import pallas as pl
from jax.experimental.pallas import tpu as pltpu
from jax.sharding import PartitionSpec as P

TILE = 128
NBANK = 4
K = 8
ROWS = 16
GROUPS = 4
MESH = pl.DeviceIdType.MESH
F32 = jnp.float32
BF16 = jnp.bfloat16
SUB = 2

NT = (((1,), (1,)), ((), ()))


def dot(a, b):
    return jnp.dot(a, b, preferred_element_type=F32)


def kernel(
    nf,
    ny,
    per_pair,
    scale,
    bnd_ref,
    x_ref,
    w_ref,
    bank_ref,
    nbr_ref,
    tid_ref,
    ew_ref,
    cnt_ref,
    cot_ref,
    act_ref,
    fg_ref,
    wg_ref,
    shuf,
    xk,
    out_blocks,
    land,
    near,
    an_bf,
    af_bf,
    atn_bf,
    atf_bf,
    oht_bf,
    bank_u,
    mixed,
    send_a,
    view,
    view2,
    wbuf,
    slope,
    slope_t,
    slope2,
    send_g,
    cols,
    back,
    own,
    send_d,
    land_d,
    part,
    right_s,
    right_r,
    left_s,
    left_r,
    send_z,
    land_z,
    send_y,
    land_y,
    phase_s,
    phase_r,
    wring_s,
    wring_r,
    wpair_s,
    wpair_r,
    gring_s,
    gring_r,
):
    nb = nf
    chips = nf // 2
    chunk = nf * ROWS // ny
    per_chunk = chunk // ROWS
    half = chips * ROWS
    far = ny * ROWS
    lanes = NBANK * nb
    group = ROWS // GROUPS
    width = group * TILE
    right = ny // 2
    left = ny - 1 - right

    me = lax.axis_index("feat")
    dom = lax.axis_index("dom")
    core = lax.rem(me, 2)
    chip = lax.div(me, 2)
    partner = me + 1 - 2 * core

    def at_dom(step):
        return lax.rem(dom + step + ny, ny)

    def copy_to(src, dst, send_sem, recv_sem, feat_id, dom_id):
        return pltpu.make_async_remote_copy(
            src_ref=src,
            dst_ref=dst,
            send_sem=send_sem,
            recv_sem=recv_sem,
            device_id=(feat_id, dom_id),
            device_id_type=MESH,
        )

    def wait_bytes(ref, sem):
        pltpu.make_async_copy(ref, ref, sem).wait()

    barrier = pltpu.get_barrier_semaphore()

    def greet_dom(step, carry):
        pl.semaphore_signal(
            barrier, inc=1, device_id=(me, at_dom(step)), device_id_type=MESH
        )
        return carry

    def greet_feat(step, carry):
        pl.semaphore_signal(
            barrier, inc=1, device_id=(lax.rem(me + step, nf), dom), device_id_type=MESH
        )
        return carry

    lax.fori_loop(1, ny, greet_dom, 0)
    lax.fori_loop(1, nf, greet_feat, 0)

    for b in range(nb):
        shuf[b * ROWS : (b + 1) * ROWS, :] = x_ref[
            :, b * TILE : (b + 1) * TILE
        ].astype(F32)
    for f in range(ROWS):
        xk[f // group, :, (f % group) * TILE : (f % group + 1) * TILE] = shuf[
            pl.ds(f, nb, stride=ROWS), :
        ].astype(BF16)

    lane = lax.broadcasted_iota(jnp.int32, (1, far), 1)
    lane_q = lax.div(lane, ROWS)
    lane_g = lax.rem(lax.div(lane, per_pair), GROUPS)
    lane_j = lax.rem(lane, per_pair)
    wanted = jnp.full((1, far), -1, jnp.int32)
    for q in range(ny):
        for j in range(per_pair):
            wanted = jnp.where(
                (lane_q == q) & (lane_j == j), bnd_ref[j, q], wanted
            )
    row_b = lax.broadcasted_iota(jnp.int32, (nb, far), 0)
    hots = [
        jnp.where((row_b == wanted) & (lane_g == g), 1.0, 0.0) for g in range(GROUPS)
    ]
    for g in range(GROUPS):
        oht_bf[g] = hots[g].astype(BF16)
    hot = jnp.concatenate(hots, axis=0).T.astype(BF16)
    out_blocks[...] = (
        dot(hot, xk[...].reshape(GROUPS * nb, width))
        .astype(BF16)
        .reshape(ny, ROWS, width)
    )

    pl.semaphore_wait(barrier, nf + ny - 2)

    def send_blocks(step, carry):
        to = at_dom(step)
        copy_to(
            out_blocks.at[to], land.at[dom], phase_s.at[0], phase_r.at[0], me, to
        ).start()
        return carry

    lax.fori_loop(1, ny, send_blocks, 0)

    my_rows = pl.ds(pl.multiple_of(chip * ROWS, ROWS), ROWS)
    my_chunk = pl.ds(pl.multiple_of(dom * chunk, chunk), chunk)

    def send_weight(step, carry):
        to = lax.rem(me + 2 * step, nf)
        copy_to(
            w_ref.at[:, my_chunk],
            wbuf.at[dom, core, my_rows, :],
            phase_s.at[1],
            phase_r.at[1],
            to,
            dom,
        ).start()
        return carry

    lax.fori_loop(1, chips, send_weight, 0)
    wbuf[dom, core, my_rows, :] = w_ref[:, my_chunk]
    land[dom] = out_blocks[dom]

    for t in range(NBANK):
        bank_u[:, t * TILE : (t + 1) * TILE] = bank_ref[t]
    nbr = jnp.concatenate([nbr_ref[...]] * NBANK, axis=1)
    tid = jnp.concatenate([tid_ref[...]] * NBANK, axis=1)
    edge = jnp.concatenate([ew_ref[...].astype(F32)] * NBANK, axis=1)
    cnt = jnp.concatenate([cnt_ref[...]] * NBANK, axis=1)
    lane_t = lax.div(lax.broadcasted_iota(jnp.int32, (K, lanes), 1), nb)
    slot = lax.broadcasted_iota(jnp.int32, (K, lanes), 0)
    coeff = jnp.where((tid == lane_t) & (slot < cnt), edge, 0.0)
    near_c = lax.broadcasted_iota(jnp.int32, (nb, lanes), 0)
    far_l = lax.broadcasted_iota(jnp.int32, (far, lanes), 0)
    far_c = nb + lax.div(far_l, ROWS) * per_pair + lax.rem(far_l, per_pair)
    at_near = jnp.zeros((nb, lanes), F32)
    at_far = jnp.zeros((far, lanes), F32)
    for k in range(K):
        at_near += jnp.where(near_c == nbr[k : k + 1], coeff[k : k + 1], 0.0)
        at_far += jnp.where(far_c == nbr[k : k + 1], coeff[k : k + 1], 0.0)
    near_hi = at_near.astype(BF16).astype(F32)
    far_hi = at_far.astype(BF16).astype(F32)
    near_2 = jnp.concatenate([near_hi, at_near - near_hi], axis=0)
    far_2 = jnp.concatenate([far_hi, at_far - far_hi], axis=0)
    atn_bf[...] = near_2.astype(BF16)
    atf_bf[...] = far_2.astype(BF16)
    an_bf[...] = near_2.T.astype(BF16)
    far_t = far_2.T
    lane_2 = lax.broadcasted_iota(jnp.int32, (lanes, 2 * far), 1)
    lane_2g = lax.rem(lax.div(lane_2, per_pair), GROUPS)
    for g in range(GROUPS):
        af_bf[g] = jnp.where(lane_2g == g, far_t, 0.0).astype(BF16)

    for g in range(GROUPS):
        near[g] = dot(an_bf[...], jnp.concatenate([xk[g]] * 2, axis=0))

    wait_bytes(wbuf.at[dom, core, pl.ds(0, half - ROWS), :], phase_r.at[1])

    def ring_right(k):
        s = at_dom(-k)
        return copy_to(
            wbuf.at[s, core],
            wbuf.at[s, core],
            wring_s.at[0, k],
            wring_r.at[0, k],
            me,
            at_dom(1),
        )

    def ring_left(k):
        s = at_dom(k)
        return copy_to(
            wbuf.at[s, core],
            wbuf.at[s, core],
            wring_s.at[1, k],
            wring_r.at[1, k],
            me,
            at_dom(-1),
        )

    def pair(s, k):
        return copy_to(
            wbuf.at[s, core],
            wbuf.at[s, core],
            wpair_s.at[k],
            wpair_r.at[k],
            partner,
            dom,
        )

    def pass_on(k):
        if 1 <= k <= right:
            wait_bytes(wbuf.at[at_dom(-k), core], wring_r.at[0, k - 1])
        if k < right:
            ring_right(k).start()
        if 1 <= k <= left:
            wait_bytes(wbuf.at[at_dom(k), core], wring_r.at[1, k - 1])
        if k < left:
            ring_left(k).start()
        if k == 0:
            pair(dom, 0).start()
        else:
            pair(at_dom(-k), k).start()
            if k <= left:
                pair(at_dom(k), right + k).start()

    pass_on(0)

    wait_bytes(land.at[pl.ds(0, ny - 1)], phase_r.at[0])
    landed = land[...].reshape(far, width)
    landed = jnp.concatenate([landed] * 2, axis=0)
    for g in range(GROUPS):
        mix = (near[g] + dot(af_bf[g], landed)).astype(BF16)
        for i in range(group):
            f = g * group + i
            for t in range(NBANK):
                mixed[f * nb : (f + 1) * nb, t * TILE : (t + 1) * TILE] = mix[
                    t * nb : (t + 1) * nb, i * TILE : (i + 1) * TILE
                ]
    for g in range(GROUPS):
        rows = group * nb
        agg = lax.dot_general(
            mixed[g * rows : (g + 1) * rows, :],
            bank_u[...],
            NT,
            preferred_element_type=F32,
        )
        for i in range(group):
            shuf[pl.ds(g * group + i, nb, stride=ROWS), :] = agg[i * nb : (i + 1) * nb]
    send_a[...] = shuf[...].astype(BF16).reshape(nb, ROWS, TILE)

    def send_agg(step, carry):
        to = lax.rem(me + step, nf)
        copy_to(
            send_a.at[to], view.at[me], phase_s.at[2], phase_r.at[2], to, dom
        ).start()
        return carry

    lax.fori_loop(1, nf, send_agg, 0)
    view[me] = send_a[me]

    for k in range(1, right + 1):
        pass_on(k)

    wait_bytes(view.at[pl.ds(0, nf - 1)], phase_r.at[2])
    view_copy = copy_to(view, view2, phase_s.at[3], phase_r.at[3], partner, dom)
    view_copy.start()

    for k in range(ny):
        s = at_dom(-k) if k <= right else at_dom(k - right)
        wait_bytes(wbuf.at[s, 1 - core], wpair_r.at[k])

    rows_all = view[...].reshape(nf * ROWS, TILE)
    for c in range(2):
        pre = jnp.zeros((half, TILE), F32)
        for s in range(0, ny, 2):
            lhs = jnp.concatenate([wbuf[s, c], wbuf[s + 1, c]], axis=1)
            pre += dot(lhs, rows_all[s * chunk : (s + 2) * chunk])
        sig = jax.nn.sigmoid(pre)
        act_ref[:, c] = (pre * sig).astype(BF16).reshape(chips, ROWS, TILE)
        cot = cot_ref[:, c].reshape(half, TILE).astype(F32)
        slo = cot * (sig * (1.0 + pre * (1.0 - sig)))
        slo = slo.astype(BF16)
        slope[c] = slo
        slope_t[:, c * half : (c + 1) * half] = slo.astype(F32).T.astype(BF16)

    slope_copy = copy_to(
        slope.at[1 - core], slope2, phase_s.at[4], phase_r.at[4], partner, dom
    )
    slope_copy.start()

    for s in range(0, ny, 2):
        lhs = jnp.concatenate(
            [
                jnp.concatenate([wbuf[s, c], wbuf[s + 1, c]], axis=1)
                for c in range(2)
            ],
            axis=0,
        )
        grad = dot(slope_t[...], lhs).T
        send_g[s * per_chunk : (s + 2) * per_chunk] = grad.astype(BF16).reshape(
            2 * per_chunk, ROWS, TILE
        )

    def send_grad(step, carry):
        to = lax.rem(me + step, nf)
        copy_to(
            send_g.at[to], cols.at[me], phase_s.at[5], phase_r.at[5], to, dom
        ).start()
        return carry

    lax.fori_loop(1, nf, send_grad, 0)
    cols[me] = send_g[me]

    wait_bytes(view2, phase_r.at[3])
    wait_bytes(slope2, phase_r.at[4])
    own_slope = jnp.concatenate([slope[core], slope2[...]], axis=1)
    sub = half // SUB

    def partial(s):
        at = pl.ds(s * per_chunk, per_chunk)
        rhs = jnp.concatenate(
            [view[at].reshape(chunk, TILE), view2[at].reshape(chunk, TILE)], axis=1
        )
        return lax.dot_general(own_slope, rhs, NT, preferred_element_type=F32)

    def ring_copy(direction, k, h):
        src, dst = ((right_s, right_r), (left_s, left_r))[direction]
        at = pl.ds(h * sub, sub)
        return copy_to(
            src.at[k, at],
            dst.at[k, at],
            gring_s.at[direction, k, h],
            gring_r.at[direction, k, h],
            me,
            at_dom(1 - 2 * direction),
        )

    right_s[0] = partial(at_dom(right)).astype(BF16)
    for h in range(SUB):
        ring_copy(0, 0, h).start()
    left_s[0] = partial(at_dom(-left)).astype(BF16)
    for h in range(SUB):
        ring_copy(1, 0, h).start()
    for k in range(1, right):
        part[k - 1] = partial(at_dom(right - k))
    for k in range(1, left):
        part[right - 1 + k - 1] = partial(at_dom(k - left))
    part[ny - 3] = partial(dom)

    def ring_step(k):
        for h in range(SUB):
            at = pl.ds(h * sub, sub)
            if k < right:
                wait_bytes(right_r.at[k - 1, at], gring_r.at[0, k - 1, h])
                right_s[k, at] = (
                    part[k - 1, at] + right_r[k - 1, at].astype(F32)
                ).astype(BF16)
                ring_copy(0, k, h).start()
            if k < left:
                wait_bytes(left_r.at[k - 1, at], gring_r.at[1, k - 1, h])
                left_s[k, at] = (
                    part[right - 2 + k, at] + left_r[k - 1, at].astype(F32)
                ).astype(BF16)
                ring_copy(1, k, h).start()

    for k in range(1, right - 1):
        ring_step(k)

    wait_bytes(cols.at[pl.ds(0, nf - 1)], phase_r.at[5])
    shuf[...] = cols[...].reshape(nb * ROWS, TILE).astype(F32)
    for g in range(GROUPS):
        lhs = jnp.concatenate(
            [shuf[pl.ds(g * group + i, nb, stride=ROWS), :] for i in range(group)],
            axis=0,
        ).astype(BF16)
        mix = dot(lhs, bank_u[...]).astype(BF16)
        for i in range(group):
            for t in range(NBANK):
                back[g, t * nb : (t + 1) * nb, i * TILE : (i + 1) * TILE] = mix[
                    i * nb : (i + 1) * nb, t * TILE : (t + 1) * TILE
                ]
    far_rows = lax.broadcasted_iota(jnp.int32, (far, width), 0)
    far_g = lax.rem(lax.div(far_rows, per_pair), GROUPS)
    sent = jnp.zeros((far, width), F32)
    for g in range(GROUPS):
        both = dot(atf_bf[...], back[g])
        sent = jnp.where(far_g == g, both[:far] + both[far:], sent)
    send_d[...] = sent.astype(BF16).reshape(ny, ROWS, width)

    def send_back(step, carry):
        to = at_dom(step)
        copy_to(
            send_d.at[to], land_d.at[dom], phase_s.at[6], phase_r.at[6], me, to
        ).start()
        return carry

    lax.fori_loop(1, ny, send_back, 0)
    land_d[dom] = send_d[dom]
    for g in range(GROUPS):
        both = dot(atn_bf[...], back[g])
        own[g] = both[:nb] + both[nb:]

    ring_step(right - 1)

    wait_bytes(land_d.at[pl.ds(0, ny - 1)], phase_r.at[6])
    landed = land_d[...].reshape(far, width)
    for g in range(GROUPS):
        total = own[g] + dot(oht_bf[g], landed)
        for i in range(group):
            shuf[pl.ds(g * group + i, nb, stride=ROWS), :] = total[
                :, i * TILE : (i + 1) * TILE
            ]
    for b in range(nb):
        fg_ref[:, b * TILE : (b + 1) * TILE] = shuf[
            b * ROWS : (b + 1) * ROWS, :
        ].astype(BF16)

    for h in range(SUB):
        at = pl.ds(h * sub, sub)
        wait_bytes(right_r.at[right - 1, at], gring_r.at[0, right - 1, h])
        wait_bytes(left_r.at[left - 1, at], gring_r.at[1, left - 1, h])
        tiles = sub // ROWS
        send_z[h * tiles : (h + 1) * tiles] = (
            (
                part[ny - 3, at]
                + right_r[right - 1, at].astype(F32)
                + left_r[left - 1, at].astype(F32)
            )
            .astype(BF16)
            .reshape(tiles, ROWS, chunk)
        )

    def send_rows(step, carry):
        to = lax.rem(chip + step, chips)
        copy_to(
            send_z.at[to],
            land_z.at[chip],
            phase_s.at[7],
            phase_r.at[7],
            2 * to + core,
            dom,
        ).start()
        return carry

    lax.fori_loop(1, chips, send_rows, 0)
    land_z[chip] = send_z[chip]
    wait_bytes(land_z.at[pl.ds(0, chips - 1)], phase_r.at[7])
    rows_sum = land_z[0].astype(F32)
    for m in range(1, chips):
        rows_sum += land_z[m].astype(F32)
    send_y[...] = rows_sum * scale

    def send_out(step, carry):
        to = at_dom(step)
        copy_to(send_y, land_y.at[dom], phase_s.at[8], phase_r.at[8], me, to).start()
        return carry

    lax.fori_loop(1, ny, send_out, 0)
    land_y[dom] = send_y[...]
    wait_bytes(land_y.at[pl.ds(0, ny - 1)], phase_r.at[8])
    for s in range(ny):
        wg_ref[:, s * chunk : (s + 1) * chunk] = land_y[s]

    wait_bytes(out_blocks.at[pl.ds(0, ny - 1)], phase_s.at[0])
    wait_bytes(wbuf.at[0, 0, pl.ds(0, half - ROWS), :], phase_s.at[1])
    wait_bytes(send_a.at[pl.ds(0, nf - 1)], phase_s.at[2])
    view_copy.wait_send()
    slope_copy.wait_send()
    wait_bytes(send_g.at[pl.ds(0, nf - 1)], phase_s.at[5])
    wait_bytes(send_d.at[pl.ds(0, ny - 1)], phase_s.at[6])
    wait_bytes(send_z.at[pl.ds(0, chips - 1)], phase_s.at[7])
    wait_bytes(land_y.at[pl.ds(0, ny - 1)], phase_s.at[8])
    for k in range(right):
        ring_right(k).wait_send()
        for h in range(SUB):
            ring_copy(0, k, h).wait_send()
    for k in range(left):
        ring_left(k).wait_send()
        for h in range(SUB):
            ring_copy(1, k, h).wait_send()
    for k in range(ny):
        pair(dom, k).wait_send()


def per_device(
    nf,
    ny,
    features,
    weight,
    tile_bank,
    neighbors,
    tile_ids,
    edge_weight,
    counts,
    boundary,
    cotangent,
):
    nb = features.shape[2] // TILE
    per_pair = boundary.shape[2]
    chips = nf // 2
    half = chips * ROWS
    chunk = nf * ROWS // ny
    far = ny * ROWS
    lanes = NBANK * nb
    width = ROWS // GROUPS * TILE
    right = ny // 2
    left = ny - 1 - right
    scale = 1.0 / math.sqrt(ny * features.shape[2])
    vmem = pl.BlockSpec(memory_space=pltpu.VMEM)
    dma = pltpu.SemaphoreType.DMA
    act, feature_grad, weight_grad = pl.pallas_call(
        functools.partial(kernel, nf, ny, per_pair, scale),
        out_shape=(
            jax.ShapeDtypeStruct((chips, 2, ROWS, TILE), BF16),
            jax.ShapeDtypeStruct((ROWS, nb * TILE), BF16),
            jax.ShapeDtypeStruct((ROWS, nf * ROWS), F32),
        ),
        in_specs=[pl.BlockSpec(memory_space=pltpu.SMEM)] + [vmem] * 8,
        out_specs=(vmem, vmem, vmem),
        scratch_shapes=[
            pltpu.VMEM((nb * ROWS, TILE), F32),
            pltpu.VMEM((GROUPS, nb, width), BF16),
            pltpu.VMEM((ny, ROWS, width), BF16),
            pltpu.VMEM((ny, ROWS, width), BF16),
            pltpu.VMEM((GROUPS, lanes, width), F32),
            pltpu.VMEM((lanes, 2 * nb), BF16),
            pltpu.VMEM((GROUPS, lanes, 2 * far), BF16),
            pltpu.VMEM((2 * nb, lanes), BF16),
            pltpu.VMEM((2 * far, lanes), BF16),
            pltpu.VMEM((GROUPS, nb, far), BF16),
            pltpu.VMEM((TILE, NBANK * TILE), BF16),
            pltpu.VMEM((ROWS * nb, NBANK * TILE), BF16),
            pltpu.VMEM((nb, ROWS, TILE), BF16),
            pltpu.VMEM((nf, ROWS, TILE), BF16),
            pltpu.VMEM((nf, ROWS, TILE), BF16),
            pltpu.VMEM((ny, 2, half, chunk), BF16),
            pltpu.VMEM((2, half, TILE), BF16),
            pltpu.VMEM((TILE, 2 * half), BF16),
            pltpu.VMEM((half, TILE), BF16),
            pltpu.VMEM((nf, ROWS, TILE), BF16),
            pltpu.VMEM((nf, ROWS, TILE), BF16),
            pltpu.VMEM((GROUPS, lanes, width), BF16),
            pltpu.VMEM((GROUPS, nb, width), F32),
            pltpu.VMEM((ny, ROWS, width), BF16),
            pltpu.VMEM((ny, ROWS, width), BF16),
            pltpu.VMEM((ny - 2, half, chunk), F32),
            pltpu.VMEM((right, half, chunk), BF16),
            pltpu.VMEM((right, half, chunk), BF16),
            pltpu.VMEM((left, half, chunk), BF16),
            pltpu.VMEM((left, half, chunk), BF16),
            pltpu.VMEM((chips, ROWS, chunk), BF16),
            pltpu.VMEM((chips, ROWS, chunk), BF16),
            pltpu.VMEM((ROWS, chunk), F32),
            pltpu.VMEM((ny, ROWS, chunk), F32),
            dma((9,)),
            dma((9,)),
            dma((2, right)),
            dma((2, right)),
            dma((ny,)),
            dma((ny,)),
            dma((2, right, SUB)),
            dma((2, right, SUB)),
        ],
        compiler_params=pltpu.CompilerParams(
            collective_id=0,
            has_side_effects=True,
            vmem_limit_bytes=48 * 2**20,
        ),
    )(
        boundary[:, 0, :].T,
        features[0],
        weight,
        tile_bank,
        neighbors[0].T,
        tile_ids[0].T,
        edge_weight[0].T,
        counts,
        cotangent[0].reshape(chips, 2, ROWS, TILE),
    )
    return (
        act.reshape(cotangent.shape),
        feature_grad[None],
        weight_grad,
    )


def solution(mesh):
    in_specs = (
        P("dom", "feat", None),
        P("feat", None),
        P(),
        P("dom", None, None),
        P("dom", None, None),
        P("dom", None, None),
        P("dom", None),
        P(None, "dom", None),
        P("dom", None, "feat"),
    )
    out_specs = (P("dom", None, "feat"), P("dom", "feat", None), P("feat", None))
    return jax.shard_map(
        functools.partial(per_device, mesh.shape["feat"], mesh.shape["dom"]),
        mesh=mesh,
        in_specs=in_specs,
        out_specs=out_specs,
        check_vma=False,
    )
```

```python
import functools
import math

import jax
import jax.numpy as jnp
from jax import lax
from jax.experimental import pallas as pl
from jax.experimental.pallas import tpu as pltpu
from jax.sharding import PartitionSpec as P

TILE = 128
NBANK = 4
K = 8
ROWS = 16
GROUPS = 4
MESH = pl.DeviceIdType.MESH
F32 = jnp.float32
BF16 = jnp.bfloat16
NX = 4

NT = (((1,), (1,)), ((), ()))


def dot(a, b):
    return jnp.dot(a, b, preferred_element_type=F32)


def kernel(
    nf,
    ny,
    per_pair,
    scale,
    bnd_hbm,
    x_hbm,
    w_hbm,
    bank_hbm,
    nbr_hbm,
    tid_hbm,
    ew_hbm,
    cnt_hbm,
    cot_hbm,
    act_hbm,
    fg_hbm,
    wg_hbm,
    act_ref,
    fg_ref,
    wg_ref,
    bnd_ref,
    x_ref,
    bank_ref,
    nbr_ref,
    tid_ref,
    ew_ref,
    cnt_ref,
    cot_ref,
    shuf,
    xk,
    out_blocks,
    land,
    near,
    an_bf,
    af_bf,
    atn_bf,
    atf_bf,
    oht_bf,
    bank_u,
    mixed,
    send_a,
    view,
    view2,
    wbuf,
    slope,
    slope_t,
    slope2,
    send_g,
    cols,
    back,
    own,
    send_d,
    land_d,
    send_x,
    land_x,
    send_z,
    land_z,
    send_y,
    land_y,
    in_sem,
    go_sem,
    phase_s,
    phase_r,
    wz_s,
    wz_r,
    wx_s,
    wx_r,
    wp_s,
    wp_r,
    gx_s,
    gx_r,
):
    nb = nf
    nx = NX
    nz = nf // (2 * nx)
    chips = nf // 2
    chunk = nf * ROWS // ny
    per_chunk = chunk // ROWS
    half = chips * ROWS
    far = ny * ROWS
    lanes = NBANK * nb
    group = ROWS // GROUPS
    width = group * TILE

    me = lax.axis_index("feat")
    dom = lax.axis_index("dom")
    core = lax.rem(me, 2)
    col = lax.rem(lax.div(me, 2), nx)
    row = lax.div(me, 2 * nx)
    partner = me + 1 - 2 * core

    def device(z, x, c):
        return (z * nx + x) * 2 + c

    def at_dom(step):
        return lax.rem(dom + step + ny, ny)

    def at_row(step):
        return lax.rem(row + step + nz, nz)

    def at_col(step):
        return lax.rem(col + step + nx, nx)

    def copy_to(src, dst, send_sem, recv_sem, feat_id, dom_id):
        return pltpu.make_async_remote_copy(
            src_ref=src,
            dst_ref=dst,
            send_sem=send_sem,
            recv_sem=recv_sem,
            device_id=(feat_id, dom_id),
            device_id_type=MESH,
        )

    def wait_bytes(ref, sem):
        pltpu.make_async_copy(ref, ref, sem).wait()

    barrier = pltpu.get_barrier_semaphore()

    def greet(feat_id, dom_id):
        pl.semaphore_signal(
            barrier, inc=1, device_id=(feat_id, dom_id), device_id_type=MESH
        )

    for step in range(1, ny):
        greet(me, at_dom(step))
    for step in range(1, nz):
        greet(device(at_row(step), col, core), dom)
    for step in range(1, 2 * nx):
        greet(row * (2 * nx) + lax.rem(lax.rem(me, 2 * nx) + step, 2 * nx), dom)

    fetches = [
        pltpu.make_async_copy(src, dst, in_sem.at[i])
        for i, (src, dst) in enumerate(
            (
                (x_hbm, x_ref),
                (bnd_hbm, bnd_ref),
                (w_hbm, wbuf.at[core, row, col]),
                (nbr_hbm, nbr_ref),
                (tid_hbm, tid_ref),
                (ew_hbm, ew_ref),
                (cnt_hbm, cnt_ref),
                (bank_hbm, bank_ref),
                (cot_hbm, cot_ref),
            )
        )
    ]
    for fetch in fetches:
        fetch.start()
    for fetch in fetches[:3]:
        fetch.wait()

    for b in range(nb):
        shuf[b * ROWS : (b + 1) * ROWS, :] = x_ref[
            :, b * TILE : (b + 1) * TILE
        ].astype(F32)
    for f in range(ROWS):
        xk[f // group, :, (f % group) * TILE : (f % group + 1) * TILE] = shuf[
            pl.ds(f, nb, stride=ROWS), :
        ].astype(BF16)

    lane = lax.broadcasted_iota(jnp.int32, (per_pair, far), 1)
    spread = jnp.full((per_pair, far), -1, jnp.int32)
    for q in range(ny):
        spread = jnp.where(
            lax.div(lane, ROWS) == q, bnd_ref[:, q : q + 1], spread
        )
    lane = lax.broadcasted_iota(jnp.int32, (1, far), 1)
    lane_g = lax.rem(lax.div(lane, per_pair), GROUPS)
    lane_j = lax.rem(lane, per_pair)
    wanted = spread[0:1]
    for j in range(1, per_pair):
        wanted = jnp.where(lane_j == j, spread[j : j + 1], wanted)
    row_b = lax.broadcasted_iota(jnp.int32, (nb, far), 0)
    hots = [
        jnp.where((row_b == wanted) & (lane_g == g), 1.0, 0.0) for g in range(GROUPS)
    ]
    for g in range(GROUPS):
        oht_bf[g] = hots[g].astype(BF16)
    hot = jnp.concatenate(hots, axis=0).T.astype(BF16)
    out_blocks[...] = (
        dot(hot, xk[...].reshape(GROUPS * nb, width))
        .astype(BF16)
        .reshape(ny, ROWS, width)
    )

    pl.semaphore_wait(barrier, ny - 1 + nz - 1 + 2 * nx - 1)

    for step in range(1, nz):
        pl.semaphore_signal(
            go_sem,
            inc=1,
            device_id=(device(at_row(step), col, core), dom),
            device_id_type=MESH,
        )

    for step in range(1, ny):
        to = at_dom(step)
        copy_to(
            out_blocks.at[to], land.at[dom], phase_s.at[0], phase_r.at[0], me, to
        ).start()

    def weight_z(step):
        block = wbuf.at[core, row, col]
        return copy_to(
            block,
            block,
            wz_s.at[step],
            wz_r.at[step],
            device(at_row(step), col, core),
            dom,
        )

    def weight_x(step, aside):
        block = wbuf.at[core, at_row(-step), col]
        return copy_to(
            block,
            block,
            wx_s.at[step],
            wx_r.at[step],
            device(row, at_col(aside), core),
            dom,
        )

    def weight_pair(step):
        blocks = wbuf.at[core, at_row(-step)]
        return copy_to(blocks, blocks, wp_s.at[step], wp_r.at[step], partner, dom)

    order = [0]
    for step in range(1, nz // 2 + 1):
        order.append(step)
        if nz - step != step:
            order.append(nz - step)

    def forward_x(step):
        if step:
            wait_bytes(wbuf.at[core, at_row(-step), col], wz_r.at[step])
        for aside in range(1, nx):
            weight_x(step, aside).start()

    def forward_pair(step):
        wait_bytes(wbuf.at[core, at_row(-step), pl.ds(0, nx - 1)], wx_r.at[step])
        weight_pair(step).start()

    forward_x(0)
    for step in order[1:]:
        weight_z(step).start()
    land[dom] = out_blocks[dom]

    for fetch in fetches[3:]:
        fetch.wait()
    for t in range(NBANK):
        bank_u[:, t * TILE : (t + 1) * TILE] = bank_ref[t]
    nbr = jnp.concatenate([nbr_ref[...]] * NBANK, axis=1)
    tid = jnp.concatenate([tid_ref[...]] * NBANK, axis=1)
    edge = jnp.concatenate([ew_ref[...].astype(F32)] * NBANK, axis=1)
    cnt = jnp.concatenate([cnt_ref[...]] * NBANK, axis=1)
    lane_t = lax.div(lax.broadcasted_iota(jnp.int32, (K, lanes), 1), nb)
    slot = lax.broadcasted_iota(jnp.int32, (K, lanes), 0)
    coeff = jnp.where((tid == lane_t) & (slot < cnt), edge, 0.0)
    near_c = lax.broadcasted_iota(jnp.int32, (nb, lanes), 0)
    far_l = lax.broadcasted_iota(jnp.int32, (far, lanes), 0)
    far_c = nb + lax.div(far_l, ROWS) * per_pair + lax.rem(far_l, per_pair)
    at_near = jnp.zeros((nb, lanes), F32)
    at_far = jnp.zeros((far, lanes), F32)
    for k in range(K):
        at_near += jnp.where(near_c == nbr[k : k + 1], coeff[k : k + 1], 0.0)
        at_far += jnp.where(far_c == nbr[k : k + 1], coeff[k : k + 1], 0.0)
    near_hi = at_near.astype(BF16).astype(F32)
    far_hi = at_far.astype(BF16).astype(F32)
    near_2 = jnp.concatenate([near_hi, at_near - near_hi], axis=0)
    far_2 = jnp.concatenate([far_hi, at_far - far_hi], axis=0)
    atn_bf[...] = near_2.astype(BF16)
    atf_bf[...] = far_2.astype(BF16)
    an_bf[...] = near_2.T.astype(BF16)
    far_t = far_2.T
    lane_2 = lax.broadcasted_iota(jnp.int32, (lanes, 2 * far), 1)
    lane_2g = lax.rem(lax.div(lane_2, per_pair), GROUPS)
    for g in range(GROUPS):
        af_bf[g] = jnp.where(lane_2g == g, far_t, 0.0).astype(BF16)

    for g in range(GROUPS):
        near[g] = dot(an_bf[...], jnp.concatenate([xk[g]] * 2, axis=0))

    for step in order[1:3]:
        forward_x(step)

    wait_bytes(land.at[pl.ds(0, ny - 1)], phase_r.at[0])
    landed = land[...].reshape(far, width)
    landed = jnp.concatenate([landed] * 2, axis=0)
    for g in range(GROUPS):
        mix = (near[g] + dot(af_bf[g], landed)).astype(BF16)
        for i in range(group):
            f = g * group + i
            for t in range(NBANK):
                mixed[f * nb : (f + 1) * nb, t * TILE : (t + 1) * TILE] = mix[
                    t * nb : (t + 1) * nb, i * TILE : (i + 1) * TILE
                ]
    for g in range(GROUPS):
        rows = group * nb
        agg = lax.dot_general(
            mixed[g * rows : (g + 1) * rows, :],
            bank_u[...],
            NT,
            preferred_element_type=F32,
        )
        for i in range(group):
            shuf[pl.ds(g * group + i, nb, stride=ROWS), :] = agg[i * nb : (i + 1) * nb]
    send_a[...] = shuf[...].astype(BF16).reshape(nb, ROWS, TILE)

    pl.semaphore_wait(go_sem, nz - 1)

    def send_agg(step, carry):
        to = lax.rem(me + step, nf)
        copy_to(
            send_a.at[to], view.at[me], phase_s.at[1], phase_r.at[1], to, dom
        ).start()
        return carry

    lax.fori_loop(1, nf, send_agg, 0)
    view[me] = send_a[me]

    for step in order[3:]:
        forward_x(step)
    for step in order:
        forward_pair(step)

    wait_bytes(view.at[pl.ds(0, nf - 1)], phase_r.at[1])
    view_copy = copy_to(view, view2, phase_s.at[2], phase_r.at[2], partner, dom)
    view_copy.start()

    rows_all = view[...].reshape(nf * ROWS, TILE)
    for turn in range(2):
        c = core if turn == 0 else 1 - core
        if turn == 1:
            for step in order:
                wait_bytes(wbuf.at[1 - core, at_row(-step)], wp_r.at[step])
        pre = dot(wbuf[c].reshape(half, nf * ROWS), rows_all)
        sig = jax.nn.sigmoid(pre)
        act_ref[:, c] = (pre * sig).astype(BF16).reshape(chips, ROWS, TILE)
        cot = cot_ref[:, c].reshape(half, TILE).astype(F32)
        slo = cot * (sig * (1.0 + pre * (1.0 - sig)))
        slo = slo.astype(BF16)
        slope[c] = slo

    slope_copy = copy_to(
        slope.at[1 - core], slope2, phase_s.at[3], phase_r.at[3], partner, dom
    )
    slope_copy.start()
    act_out = pltpu.make_async_copy(act_ref, act_hbm, in_sem.at[9])
    act_out.start()

    for c in range(2):
        slope_t[:, c * half : (c + 1) * half] = slope[c].astype(F32).T.astype(BF16)
    piece = 2 * chunk
    for s in range(0, ny, 2):
        at = slice(s * chunk, (s + 2) * chunk)
        lhs = jnp.concatenate(
            [wbuf[c, :, :, :, at].reshape(half, piece) for c in range(2)], axis=0
        )
        grad = dot(slope_t[...], lhs).T
        send_g[s * per_chunk : (s + 2) * per_chunk] = grad.astype(BF16).reshape(
            2 * per_chunk, ROWS, TILE
        )

    def send_grad(step, carry):
        to = lax.rem(me + step, nf)
        copy_to(
            send_g.at[to], cols.at[me], phase_s.at[4], phase_r.at[4], to, dom
        ).start()
        return carry

    lax.fori_loop(1, nf, send_grad, 0)
    cols[me] = send_g[me]

    wait_bytes(view2, phase_r.at[2])
    wait_bytes(slope2, phase_r.at[3])
    own_slope = jnp.concatenate([slope[core], slope2[...]], axis=1)

    def partial_x(k, aside):
        to = at_col(aside)
        return copy_to(
            send_x.at[k, to],
            land_x.at[k, aside - 1],
            gx_s.at[k],
            gx_r.at[k],
            device(row, to, core),
            dom,
        )

    for k in range(ny):
        at = pl.ds(at_dom(k) * per_chunk, per_chunk)
        rhs = jnp.concatenate(
            [view[at].reshape(chunk, TILE), view2[at].reshape(chunk, TILE)], axis=1
        )
        part = lax.dot_general(own_slope, rhs, NT, preferred_element_type=F32)
        part = part.astype(BF16).reshape(nz, nx, ROWS, chunk)
        for x in range(nx):
            send_x[k, x] = part[:, x]
        for aside in range(1, nx):
            partial_x(k, aside).start()

    def spread_out(k):
        to = at_dom(k)
        wait_bytes(land_x.at[k], gx_r.at[k])
        total = send_x[k, col].astype(F32)
        for aside in range(1, nx):
            total += land_x[k, aside - 1].astype(F32)
        send_z[k] = total.astype(BF16)
        for step in range(nz):
            if k == 0 and step == 0:
                continue
            z = at_row(step)
            copy_to(
                send_z.at[k, z],
                land_z.at[row * ny + dom],
                phase_s.at[5],
                phase_r.at[5],
                device(z, col, core),
                to,
            ).start()

    for k in range(ny // 2):
        spread_out(k)

    wait_bytes(cols.at[pl.ds(0, nf - 1)], phase_r.at[4])
    shuf[...] = cols[...].reshape(nb * ROWS, TILE).astype(F32)
    for g in range(GROUPS):
        lhs = jnp.concatenate(
            [shuf[pl.ds(g * group + i, nb, stride=ROWS), :] for i in range(group)],
            axis=0,
        ).astype(BF16)
        mix = dot(lhs, bank_u[...]).astype(BF16)
        for i in range(group):
            for t in range(NBANK):
                back[g, t * nb : (t + 1) * nb, i * TILE : (i + 1) * TILE] = mix[
                    i * nb : (i + 1) * nb, t * TILE : (t + 1) * TILE
                ]
    far_rows = lax.broadcasted_iota(jnp.int32, (far, width), 0)
    far_g = lax.rem(lax.div(far_rows, per_pair), GROUPS)
    sent = jnp.zeros((far, width), F32)
    for g in range(GROUPS):
        both = dot(atf_bf[...], back[g])
        sent = jnp.where(far_g == g, both[:far] + both[far:], sent)
    send_d[...] = sent.astype(BF16).reshape(ny, ROWS, width)

    for step in range(1, ny):
        to = at_dom(step)
        copy_to(
            send_d.at[to], land_d.at[dom], phase_s.at[6], phase_r.at[6], me, to
        ).start()
    land_d[dom] = send_d[dom]

    for k in range(ny // 2, ny):
        spread_out(k)
    land_z[row * ny + dom] = send_z[0, row]

    for g in range(GROUPS):
        both = dot(atn_bf[...], back[g])
        own[g] = both[:nb] + both[nb:]

    wait_bytes(land_d.at[pl.ds(0, ny - 1)], phase_r.at[6])
    landed = land_d[...].reshape(far, width)
    for g in range(GROUPS):
        total = own[g] + dot(oht_bf[g], landed)
        for i in range(group):
            shuf[pl.ds(g * group + i, nb, stride=ROWS), :] = total[
                :, i * TILE : (i + 1) * TILE
            ]
    for b in range(nb):
        fg_ref[:, b * TILE : (b + 1) * TILE] = shuf[
            b * ROWS : (b + 1) * ROWS, :
        ].astype(BF16)

    fg_out = pltpu.make_async_copy(fg_ref, fg_hbm, in_sem.at[10])
    fg_out.start()

    wait_bytes(land_z.at[pl.ds(0, nz * ny - 1)], phase_r.at[5])
    rows_sum = land_z[0].astype(F32)
    for m in range(1, nz * ny):
        rows_sum += land_z[m].astype(F32)
    send_y[...] = rows_sum * scale
    for step in range(1, ny):
        to = at_dom(step)
        copy_to(send_y, land_y.at[dom], phase_s.at[7], phase_r.at[7], me, to).start()
    land_y[dom] = send_y[...]

    wait_bytes(out_blocks.at[pl.ds(0, ny - 1)], phase_s.at[0])
    wait_bytes(send_a.at[pl.ds(0, nf - 1)], phase_s.at[1])
    view_copy.wait_send()
    slope_copy.wait_send()
    wait_bytes(send_g.at[pl.ds(0, nf - 1)], phase_s.at[4])
    wait_bytes(land_z.at[pl.ds(0, nz * ny - 1)], phase_s.at[5])
    wait_bytes(send_d.at[pl.ds(0, ny - 1)], phase_s.at[6])
    for step in order:
        if step:
            weight_z(step).wait_send()
        wait_bytes(wbuf.at[0, 0, pl.ds(0, nx - 1)], wx_s.at[step])
        weight_pair(step).wait_send()
    for k in range(ny):
        wait_bytes(land_x.at[k], gx_s.at[k])

    wait_bytes(land_y.at[pl.ds(0, ny - 1)], phase_r.at[7])
    for s in range(ny):
        wg_ref[:, s * chunk : (s + 1) * chunk] = land_y[s]
    wg_out = pltpu.make_async_copy(wg_ref, wg_hbm, in_sem.at[11])
    wg_out.start()
    act_out.wait()
    fg_out.wait()
    wg_out.wait()
    wait_bytes(land_y.at[pl.ds(0, ny - 1)], phase_s.at[7])


def per_device(
    nf,
    ny,
    features,
    weight,
    tile_bank,
    neighbors,
    tile_ids,
    edge_weight,
    counts,
    boundary,
    cotangent,
):
    nb = features.shape[2] // TILE
    per_pair = boundary.shape[2]
    nx = NX
    nz = nf // (2 * nx)
    chips = nf // 2
    half = chips * ROWS
    chunk = nf * ROWS // ny
    far = ny * ROWS
    lanes = NBANK * nb
    width = ROWS // GROUPS * TILE
    scale = 1.0 / math.sqrt(ny * features.shape[2])
    hbm = pl.BlockSpec(memory_space=pl.ANY)
    dma = pltpu.SemaphoreType.DMA
    act, feature_grad, weight_grad = pl.pallas_call(
        functools.partial(kernel, nf, ny, per_pair, scale),
        out_shape=(
            jax.ShapeDtypeStruct((chips, 2, ROWS, TILE), BF16),
            jax.ShapeDtypeStruct((ROWS, nb * TILE), BF16),
            jax.ShapeDtypeStruct((ROWS, nf * ROWS), F32),
        ),
        in_specs=[hbm] * 9,
        out_specs=(hbm, hbm, hbm),
        scratch_shapes=[
            pltpu.VMEM((chips, 2, ROWS, TILE), BF16),
            pltpu.VMEM((ROWS, nb * TILE), BF16),
            pltpu.VMEM((ROWS, nf * ROWS), F32),
            pltpu.VMEM((per_pair, ny), jnp.int32),
            pltpu.VMEM((ROWS, nb * TILE), BF16),
            pltpu.VMEM((NBANK, TILE, TILE), BF16),
            pltpu.VMEM((K, nb), jnp.int32),
            pltpu.VMEM((K, nb), jnp.int32),
            pltpu.VMEM((K, nb), BF16),
            pltpu.VMEM((1, nb), jnp.int32),
            pltpu.VMEM((chips, 2, ROWS, TILE), BF16),
            pltpu.VMEM((nb * ROWS, TILE), F32),
            pltpu.VMEM((GROUPS, nb, width), BF16),
            pltpu.VMEM((ny, ROWS, width), BF16),
            pltpu.VMEM((ny, ROWS, width), BF16),
            pltpu.VMEM((GROUPS, lanes, width), F32),
            pltpu.VMEM((lanes, 2 * nb), BF16),
            pltpu.VMEM((GROUPS, lanes, 2 * far), BF16),
            pltpu.VMEM((2 * nb, lanes), BF16),
            pltpu.VMEM((2 * far, lanes), BF16),
            pltpu.VMEM((GROUPS, nb, far), BF16),
            pltpu.VMEM((TILE, NBANK * TILE), BF16),
            pltpu.VMEM((ROWS * nb, NBANK * TILE), BF16),
            pltpu.VMEM((nb, ROWS, TILE), BF16),
            pltpu.VMEM((nf, ROWS, TILE), BF16),
            pltpu.VMEM((nf, ROWS, TILE), BF16),
            pltpu.VMEM((2, nz, nx, ROWS, nf * ROWS), BF16),
            pltpu.VMEM((2, half, TILE), BF16),
            pltpu.VMEM((TILE, 2 * half), BF16),
            pltpu.VMEM((half, TILE), BF16),
            pltpu.VMEM((nf, ROWS, TILE), BF16),
            pltpu.VMEM((nf, ROWS, TILE), BF16),
            pltpu.VMEM((GROUPS, lanes, width), BF16),
            pltpu.VMEM((GROUPS, nb, width), F32),
            pltpu.VMEM((ny, ROWS, width), BF16),
            pltpu.VMEM((ny, ROWS, width), BF16),
            pltpu.VMEM((ny, nx, nz, ROWS, chunk), BF16),
            pltpu.VMEM((ny, nx - 1, nz, ROWS, chunk), BF16),
            pltpu.VMEM((ny, nz, ROWS, chunk), BF16),
            pltpu.VMEM((nz * ny, ROWS, chunk), BF16),
            pltpu.VMEM((ROWS, chunk), F32),
            pltpu.VMEM((ny, ROWS, chunk), F32),
            dma((12,)),
            pltpu.SemaphoreType.REGULAR,
            dma((8,)),
            dma((8,)),
            dma((nz,)),
            dma((nz,)),
            dma((nz,)),
            dma((nz,)),
            dma((nz,)),
            dma((nz,)),
            dma((ny,)),
            dma((ny,)),
        ],
        compiler_params=pltpu.CompilerParams(
            collective_id=0,
            has_side_effects=True,
            vmem_limit_bytes=60 * 2**20,
        ),
    )(
        boundary[:, 0, :].T,
        features[0],
        weight,
        tile_bank,
        neighbors[0].T,
        tile_ids[0].T,
        edge_weight[0].T,
        counts,
        cotangent[0].reshape(chips, 2, ROWS, TILE),
    )
    return (
        act.reshape(cotangent.shape),
        feature_grad[None],
        weight_grad,
    )


def solution(mesh):
    in_specs = (
        P("dom", "feat", None),
        P("feat", None),
        P(),
        P("dom", None, None),
        P("dom", None, None),
        P("dom", None, None),
        P("dom", None),
        P(None, "dom", None),
        P("dom", None, "feat"),
    )
    out_specs = (P("dom", None, "feat"), P("dom", "feat", None), P("feat", None))
    return jax.shard_map(
        functools.partial(per_device, mesh.shape["feat"], mesh.shape["dom"]),
        mesh=mesh,
        in_specs=in_specs,
        out_specs=out_specs,
        check_vma=False,
    )
```

```python
import functools
import math

import jax
import jax.numpy as jnp
from jax import lax
from jax.experimental import pallas as pl
from jax.experimental.pallas import tpu as pltpu
from jax.sharding import PartitionSpec as P

TILE = 128
NBANK = 4
K = 8
ROWS = 16
GROUPS = 4
MESH = pl.DeviceIdType.MESH
F32 = jnp.float32
BF16 = jnp.bfloat16
NX = 4
EARLY = 3
MIDDLE = 5
ZX = 4

NT = (((1,), (1,)), ((), ()))


def dot(a, b):
    return jnp.dot(a, b, preferred_element_type=F32)


def kernel(
    nf,
    ny,
    per_pair,
    scale,
    bnd_hbm,
    x_hbm,
    w_hbm,
    bank_hbm,
    nbr_hbm,
    tid_hbm,
    ew_hbm,
    cnt_hbm,
    cot_hbm,
    act_hbm,
    fg_hbm,
    wg_hbm,
    act_ref,
    fg_ref,
    wg_ref,
    bnd_ref,
    x_ref,
    bank_ref,
    nbr_ref,
    tid_ref,
    ew_ref,
    cnt_ref,
    cot_ref,
    shuf,
    xk,
    out_blocks,
    land,
    near,
    an_bf,
    af_bf,
    atn_bf,
    atf_bf,
    oht_bf,
    bank_u,
    mixed,
    send_a,
    view,
    view2,
    wbuf,
    slope,
    slope_t,
    slope2,
    send_g,
    cols,
    back,
    own,
    send_d,
    land_d,
    send_x,
    land_x,
    send_z,
    land_z,
    rest_of,
    right_s,
    right_r,
    left_s,
    left_r,
    send_w,
    land_w,
    send_y,
    land_y,
    in_sem,
    go_sem,
    phase_s,
    phase_r,
    wz_s,
    wz_r,
    wx_s,
    wx_r,
    wp_s,
    wp_r,
    gx_s,
    gx_r,
    gr_s,
    gr_r,
):
    nb = nf
    nx = NX
    nz = nf // (2 * nx)
    chips = nf // 2
    chunk = nf * ROWS // ny
    per_chunk = chunk // ROWS
    half = chips * ROWS
    far = ny * ROWS
    lanes = NBANK * nb
    group = ROWS // GROUPS
    width = group * TILE
    zx = ZX
    zy = nz - zx
    ring_tiles = zy * nx
    ring_rows = ring_tiles * ROWS
    right = ny // 2
    left = ny - 1 - right

    me = lax.axis_index("feat")
    dom = lax.axis_index("dom")
    core = lax.rem(me, 2)
    col = lax.rem(lax.div(me, 2), nx)
    row = lax.div(me, 2 * nx)
    partner = me + 1 - 2 * core

    def device(z, x, c):
        return (z * nx + x) * 2 + c

    def at_dom(step):
        return lax.rem(dom + step + ny, ny)

    def at_row(step):
        return lax.rem(row + step + nz, nz)

    def at_col(step):
        return lax.rem(col + step + nx, nx)

    def copy_to(src, dst, send_sem, recv_sem, feat_id, dom_id):
        return pltpu.make_async_remote_copy(
            src_ref=src,
            dst_ref=dst,
            send_sem=send_sem,
            recv_sem=recv_sem,
            device_id=(feat_id, dom_id),
            device_id_type=MESH,
        )

    def wait_bytes(ref, sem):
        pltpu.make_async_copy(ref, ref, sem).wait()

    barrier = pltpu.get_barrier_semaphore()

    def greet(feat_id, dom_id):
        pl.semaphore_signal(
            barrier, inc=1, device_id=(feat_id, dom_id), device_id_type=MESH
        )

    for step in range(1, ny):
        greet(me, at_dom(step))
    for step in range(1, nz):
        greet(device(at_row(step), col, core), dom)
    for step in range(1, 2 * nx):
        greet(row * (2 * nx) + lax.rem(lax.rem(me, 2 * nx) + step, 2 * nx), dom)

    fetches = [
        pltpu.make_async_copy(src, dst, in_sem.at[i])
        for i, (src, dst) in enumerate(
            (
                (x_hbm, x_ref),
                (bnd_hbm, bnd_ref),
                (w_hbm, wbuf.at[core, row, col]),
                (nbr_hbm, nbr_ref),
                (tid_hbm, tid_ref),
                (ew_hbm, ew_ref),
                (cnt_hbm, cnt_ref),
                (bank_hbm, bank_ref),
                (cot_hbm, cot_ref),
            )
        )
    ]
    for fetch in fetches:
        fetch.start()
    for fetch in fetches[:3]:
        fetch.wait()

    for b in range(nb):
        shuf[b * ROWS : (b + 1) * ROWS, :] = x_ref[
            :, b * TILE : (b + 1) * TILE
        ].astype(F32)
    for f in range(ROWS):
        xk[f // group, :, (f % group) * TILE : (f % group + 1) * TILE] = shuf[
            pl.ds(f, nb, stride=ROWS), :
        ].astype(BF16)

    lane = lax.broadcasted_iota(jnp.int32, (per_pair, far), 1)
    spread = jnp.full((per_pair, far), -1, jnp.int32)
    for q in range(ny):
        spread = jnp.where(
            lax.div(lane, ROWS) == q, bnd_ref[:, q : q + 1], spread
        )
    lane = lax.broadcasted_iota(jnp.int32, (1, far), 1)
    lane_g = lax.rem(lax.div(lane, per_pair), GROUPS)
    lane_j = lax.rem(lane, per_pair)
    wanted = spread[0:1]
    for j in range(1, per_pair):
        wanted = jnp.where(lane_j == j, spread[j : j + 1], wanted)
    row_b = lax.broadcasted_iota(jnp.int32, (nb, far), 0)
    hots = [
        jnp.where((row_b == wanted) & (lane_g == g), 1.0, 0.0) for g in range(GROUPS)
    ]
    for g in range(GROUPS):
        oht_bf[g] = hots[g].astype(BF16)
    hot = jnp.concatenate(hots, axis=0).T.astype(BF16)
    out_blocks[...] = (
        dot(hot, xk[...].reshape(GROUPS * nb, width))
        .astype(BF16)
        .reshape(ny, ROWS, width)
    )

    pl.semaphore_wait(barrier, ny - 1 + nz - 1 + 2 * nx - 1)

    for step in range(1, nz):
        pl.semaphore_signal(
            go_sem,
            inc=1,
            device_id=(device(at_row(step), col, core), dom),
            device_id_type=MESH,
        )

    for step in range(1, ny):
        to = at_dom(step)
        copy_to(
            out_blocks.at[to], land.at[dom], phase_s.at[0], phase_r.at[0], me, to
        ).start()

    def weight_z(step):
        block = wbuf.at[core, row, col]
        return copy_to(
            block,
            block,
            wz_s.at[step],
            wz_r.at[step],
            device(at_row(step), col, core),
            dom,
        )

    def weight_x(step, aside):
        block = wbuf.at[core, at_row(-step), col]
        return copy_to(
            block,
            block,
            wx_s.at[step],
            wx_r.at[step],
            device(row, at_col(aside), core),
            dom,
        )

    def weight_pair(step):
        blocks = wbuf.at[core, at_row(-step)]
        return copy_to(blocks, blocks, wp_s.at[step], wp_r.at[step], partner, dom)

    order = [0]
    for step in range(1, nz // 2 + 1):
        order.append(step)
        if nz - step != step:
            order.append(nz - step)

    def forward_x(step):
        if step:
            wait_bytes(wbuf.at[core, at_row(-step), col], wz_r.at[step])
        for aside in range(1, nx):
            weight_x(step, aside).start()

    def forward_pair(step):
        wait_bytes(wbuf.at[core, at_row(-step), pl.ds(0, nx - 1)], wx_r.at[step])
        weight_pair(step).start()

    forward_x(0)
    for step in order[1:]:
        weight_z(step).start()
    land[dom] = out_blocks[dom]

    for fetch in fetches[3:]:
        fetch.wait()
    for t in range(NBANK):
        bank_u[:, t * TILE : (t + 1) * TILE] = bank_ref[t]
    nbr = jnp.concatenate([nbr_ref[...]] * NBANK, axis=1)
    tid = jnp.concatenate([tid_ref[...]] * NBANK, axis=1)
    edge = jnp.concatenate([ew_ref[...].astype(F32)] * NBANK, axis=1)
    cnt = jnp.concatenate([cnt_ref[...]] * NBANK, axis=1)
    lane_t = lax.div(lax.broadcasted_iota(jnp.int32, (K, lanes), 1), nb)
    slot = lax.broadcasted_iota(jnp.int32, (K, lanes), 0)
    coeff = jnp.where((tid == lane_t) & (slot < cnt), edge, 0.0)
    near_c = lax.broadcasted_iota(jnp.int32, (nb, lanes), 0)
    far_l = lax.broadcasted_iota(jnp.int32, (far, lanes), 0)
    far_c = nb + lax.div(far_l, ROWS) * per_pair + lax.rem(far_l, per_pair)
    at_near = jnp.zeros((nb, lanes), F32)
    at_far = jnp.zeros((far, lanes), F32)
    for k in range(K):
        at_near += jnp.where(near_c == nbr[k : k + 1], coeff[k : k + 1], 0.0)
        at_far += jnp.where(far_c == nbr[k : k + 1], coeff[k : k + 1], 0.0)
    near_hi = at_near.astype(BF16).astype(F32)
    far_hi = at_far.astype(BF16).astype(F32)
    near_2 = jnp.concatenate([near_hi, at_near - near_hi], axis=0)
    far_2 = jnp.concatenate([far_hi, at_far - far_hi], axis=0)
    atn_bf[...] = near_2.astype(BF16)
    atf_bf[...] = far_2.astype(BF16)
    an_bf[...] = near_2.T.astype(BF16)
    far_t = far_2.T
    lane_2 = lax.broadcasted_iota(jnp.int32, (lanes, 2 * far), 1)
    lane_2g = lax.rem(lax.div(lane_2, per_pair), GROUPS)
    for g in range(GROUPS):
        af_bf[g] = jnp.where(lane_2g == g, far_t, 0.0).astype(BF16)

    for g in range(GROUPS):
        near[g] = dot(an_bf[...], jnp.concatenate([xk[g]] * 2, axis=0))

    for step in order[1:EARLY]:
        forward_x(step)

    wait_bytes(land.at[pl.ds(0, ny - 1)], phase_r.at[0])
    landed = land[...].reshape(far, width)
    landed = jnp.concatenate([landed] * 2, axis=0)
    for g in range(GROUPS):
        mix = (near[g] + dot(af_bf[g], landed)).astype(BF16)
        for i in range(group):
            f = g * group + i
            for t in range(NBANK):
                mixed[f * nb : (f + 1) * nb, t * TILE : (t + 1) * TILE] = mix[
                    t * nb : (t + 1) * nb, i * TILE : (i + 1) * TILE
                ]
    for g in range(GROUPS):
        rows = group * nb
        agg = lax.dot_general(
            mixed[g * rows : (g + 1) * rows, :],
            bank_u[...],
            NT,
            preferred_element_type=F32,
        )
        for i in range(group):
            shuf[pl.ds(g * group + i, nb, stride=ROWS), :] = agg[i * nb : (i + 1) * nb]
    send_a[...] = shuf[...].astype(BF16).reshape(nb, ROWS, TILE)

    for step in order[EARLY:MIDDLE]:
        forward_x(step)
    pl.semaphore_wait(go_sem, nz - 1)

    def send_agg(step, carry):
        to = lax.rem(me + step, nf)
        copy_to(
            send_a.at[to], view.at[me], phase_s.at[1], phase_r.at[1], to, dom
        ).start()
        return carry

    lax.fori_loop(1, nf, send_agg, 0)
    view[me] = send_a[me]

    for step in order[MIDDLE:]:
        forward_x(step)
    for step in order:
        forward_pair(step)

    wait_bytes(view.at[pl.ds(0, nf - 1)], phase_r.at[1])
    view_copy = copy_to(view, view2, phase_s.at[2], phase_r.at[2], partner, dom)
    view_copy.start()

    rows_all = view[...].reshape(nf * ROWS, TILE)
    for turn in range(2):
        c = core if turn == 0 else 1 - core
        if turn == 1:
            for step in order:
                wait_bytes(wbuf.at[1 - core, at_row(-step)], wp_r.at[step])
        pre = dot(wbuf[c].reshape(half, nf * ROWS), rows_all)
        sig = jax.nn.sigmoid(pre)
        act_ref[:, c] = (pre * sig).astype(BF16).reshape(chips, ROWS, TILE)
        cot = cot_ref[:, c].reshape(half, TILE).astype(F32)
        slo = cot * (sig * (1.0 + pre * (1.0 - sig)))
        slo = slo.astype(BF16)
        slope[c] = slo

    slope_copy = copy_to(
        slope.at[1 - core], slope2, phase_s.at[3], phase_r.at[3], partner, dom
    )
    slope_copy.start()
    act_out = pltpu.make_async_copy(act_ref, act_hbm, in_sem.at[9])
    act_out.start()

    for c in range(2):
        slope_t[:, c * half : (c + 1) * half] = slope[c].astype(F32).T.astype(BF16)
    piece = 2 * chunk
    for s in range(0, ny, 2):
        at = slice(s * chunk, (s + 2) * chunk)
        lhs = jnp.concatenate(
            [wbuf[c, :, :, :, at].reshape(half, piece) for c in range(2)], axis=0
        )
        grad = dot(slope_t[...], lhs).T
        send_g[s * per_chunk : (s + 2) * per_chunk] = grad.astype(BF16).reshape(
            2 * per_chunk, ROWS, TILE
        )

    wait_bytes(view2, phase_r.at[2])
    wait_bytes(slope2, phase_r.at[3])
    own_slope = jnp.concatenate([slope[core], slope2[...]], axis=1)

    def partial_x(k, aside):
        to = at_col(aside)
        return copy_to(
            send_x.at[k, to],
            land_x.at[k, aside - 1],
            gx_s.at[k],
            gx_r.at[k],
            device(row, to, core),
            dom,
        )

    def send_grad(step, carry):
        to = lax.rem(me + step, nf)
        copy_to(
            send_g.at[to], cols.at[me], phase_s.at[4], phase_r.at[4], to, dom
        ).start()
        return carry

    lax.fori_loop(1, nf, send_grad, 0)
    cols[me] = send_g[me]

    def ring_copy(direction, k):
        src, dst = ((right_s, right_r), (left_s, left_r))[direction]
        return copy_to(
            src.at[k],
            dst.at[k],
            gr_s.at[direction, k],
            gr_r.at[direction, k],
            me,
            at_dom(1 - 2 * direction),
        )

    def to_columns(k):
        at = pl.ds(at_dom(k) * per_chunk, per_chunk)
        rhs = jnp.concatenate(
            [view[at].reshape(chunk, TILE), view2[at].reshape(chunk, TILE)], axis=1
        )
        part = lax.dot_general(own_slope, rhs, NT, preferred_element_type=F32)
        part = part.reshape(nz, nx, ROWS, chunk)
        for x in range(nx):
            send_x[k, x] = part[:zx, x].astype(BF16)
        for aside in range(1, nx):
            partial_x(k, aside).start()
        rest = part[zx:].reshape(ring_rows, chunk)
        if k == right:
            right_s[0] = rest.astype(BF16)
            ring_copy(0, 0).start()
        elif k == right + 1:
            left_s[0] = rest.astype(BF16)
            ring_copy(1, 0).start()
        else:
            rest_of[k] = rest

    near_far = [right, right + 1]
    for k in range(1, right):
        near_far.append(right - k)
        if right + 1 + k < ny:
            near_far.append(right + 1 + k)
    near_far.append(0)
    for k in near_far:
        to_columns(k)

    def ring_step(k):
        if k < right:
            wait_bytes(right_r.at[k - 1], gr_r.at[0, k - 1])
            right_s[k] = (rest_of[right - k] + right_r[k - 1].astype(F32)).astype(BF16)
            ring_copy(0, k).start()
        if k < left:
            wait_bytes(left_r.at[k - 1], gr_r.at[1, k - 1])
            left_s[k] = (
                rest_of[right + 1 + k] + left_r[k - 1].astype(F32)
            ).astype(BF16)
            ring_copy(1, k).start()

    def spread_out(k):
        to = at_dom(k)
        wait_bytes(land_x.at[k], gx_r.at[k])
        total = send_x[k, col].astype(F32)
        for aside in range(1, nx):
            total += land_x[k, aside - 1].astype(F32)
        send_z[k] = total.astype(BF16)
        for z in range(zx):
            tile = copy_to(
                send_z.at[k, z],
                land_z.at[row * ny + dom],
                phase_s.at[5],
                phase_r.at[5],
                device(z, col, core),
                to,
            )
            if k:
                tile.start()
            else:
                pl.when(row != z)(tile.start)

    for k in near_far[:2]:
        spread_out(k)
    for k in range(1, right - 1):
        ring_step(k)

    wait_bytes(cols.at[pl.ds(0, nf - 1)], phase_r.at[4])
    shuf[...] = cols[...].reshape(nb * ROWS, TILE).astype(F32)
    for g in range(GROUPS):
        lhs = jnp.concatenate(
            [shuf[pl.ds(g * group + i, nb, stride=ROWS), :] for i in range(group)],
            axis=0,
        ).astype(BF16)
        mix = dot(lhs, bank_u[...]).astype(BF16)
        for i in range(group):
            for t in range(NBANK):
                back[g, t * nb : (t + 1) * nb, i * TILE : (i + 1) * TILE] = mix[
                    i * nb : (i + 1) * nb, t * TILE : (t + 1) * TILE
                ]
    far_rows = lax.broadcasted_iota(jnp.int32, (far, width), 0)
    far_g = lax.rem(lax.div(far_rows, per_pair), GROUPS)
    sent = jnp.zeros((far, width), F32)
    for g in range(GROUPS):
        both = dot(atf_bf[...], back[g])
        sent = jnp.where(far_g == g, both[:far] + both[far:], sent)
    send_d[...] = sent.astype(BF16).reshape(ny, ROWS, width)

    for step in range(1, ny):
        to = at_dom(step)
        copy_to(
            send_d.at[to], land_d.at[dom], phase_s.at[6], phase_r.at[6], me, to
        ).start()
    land_d[dom] = send_d[dom]

    for k in near_far[2:]:
        spread_out(k)
    if right > 1:
        ring_step(right - 1)

    @pl.when(row < zx)
    def _():
        land_z[row * ny + dom] = send_z[0, jnp.minimum(row, zx - 1)]

    for g in range(GROUPS):
        both = dot(atn_bf[...], back[g])
        own[g] = both[:nb] + both[nb:]

    wait_bytes(right_r.at[right - 1], gr_r.at[0, right - 1])
    wait_bytes(left_r.at[left - 1], gr_r.at[1, left - 1])
    send_w[...] = (
        (
            rest_of[0]
            + right_r[right - 1].astype(F32)
            + left_r[left - 1].astype(F32)
        )
        .astype(BF16)
        .reshape(ring_tiles, ROWS, chunk)
    )
    chip = row * nx + col
    for t in range(ring_tiles):
        z, x = zx + t // nx, t % nx
        tile = copy_to(
            send_w.at[t],
            land_w.at[chip],
            phase_s.at[8],
            phase_r.at[8],
            device(z, x, core),
            dom,
        )
        pl.when(chip != z * nx + x)(tile.start)

    @pl.when(row >= zx)
    def _():
        land_w[chip] = send_w[jnp.maximum(chip - zx * nx, 0)]

    wait_bytes(land_d.at[pl.ds(0, ny - 1)], phase_r.at[6])
    landed = land_d[...].reshape(far, width)
    for g in range(GROUPS):
        total = own[g] + dot(oht_bf[g], landed)
        for i in range(group):
            shuf[pl.ds(g * group + i, nb, stride=ROWS), :] = total[
                :, i * TILE : (i + 1) * TILE
            ]
    for b in range(nb):
        fg_ref[:, b * TILE : (b + 1) * TILE] = shuf[
            b * ROWS : (b + 1) * ROWS, :
        ].astype(BF16)

    fg_out = pltpu.make_async_copy(fg_ref, fg_hbm, in_sem.at[10])
    fg_out.start()

    @pl.when(row < zx)
    def _():
        wait_bytes(land_z.at[pl.ds(0, nz * ny - 1)], phase_r.at[5])
        rows_sum = land_z[0].astype(F32)
        for m in range(1, nz * ny):
            rows_sum += land_z[m].astype(F32)
        send_y[...] = rows_sum * scale

    @pl.when(row >= zx)
    def _():
        wait_bytes(land_w.at[pl.ds(0, chips - 1)], phase_r.at[8])
        rows_sum = land_w[0].astype(F32)
        for m in range(1, chips):
            rows_sum += land_w[m].astype(F32)
        send_y[...] = rows_sum * scale

    for step in range(1, ny):
        to = at_dom(step)
        copy_to(send_y, land_y.at[dom], phase_s.at[7], phase_r.at[7], me, to).start()
    land_y[dom] = send_y[...]

    wait_bytes(out_blocks.at[pl.ds(0, ny - 1)], phase_s.at[0])
    wait_bytes(send_a.at[pl.ds(0, nf - 1)], phase_s.at[1])
    view_copy.wait_send()
    slope_copy.wait_send()
    wait_bytes(send_g.at[pl.ds(0, nf - 1)], phase_s.at[4])
    @pl.when(row < zx)
    def _():
        wait_bytes(land_z.at[pl.ds(0, zx * ny - 1)], phase_s.at[5])
        wait_bytes(land_w.at[pl.ds(0, ring_tiles)], phase_s.at[8])

    @pl.when(row >= zx)
    def _():
        wait_bytes(land_z.at[pl.ds(0, zx * ny)], phase_s.at[5])
        wait_bytes(land_w.at[pl.ds(0, ring_tiles - 1)], phase_s.at[8])

    for k in range(right):
        ring_copy(0, k).wait_send()
    for k in range(left):
        ring_copy(1, k).wait_send()
    wait_bytes(send_d.at[pl.ds(0, ny - 1)], phase_s.at[6])
    for step in order:
        if step:
            weight_z(step).wait_send()
        wait_bytes(wbuf.at[0, 0, pl.ds(0, nx - 1)], wx_s.at[step])
        weight_pair(step).wait_send()
    for k in range(ny):
        wait_bytes(land_x.at[k], gx_s.at[k])

    wait_bytes(land_y.at[pl.ds(0, ny - 1)], phase_r.at[7])
    for s in range(ny):
        wg_ref[:, s * chunk : (s + 1) * chunk] = land_y[s]
    wg_out = pltpu.make_async_copy(wg_ref, wg_hbm, in_sem.at[11])
    wg_out.start()
    act_out.wait()
    fg_out.wait()
    wg_out.wait()
    wait_bytes(land_y.at[pl.ds(0, ny - 1)], phase_s.at[7])


def hand_over(*refs):
    n = len(refs) // 3
    ins, outs, held, sem = refs[:n], refs[n : 2 * n], refs[2 * n : 3 * n], refs[-1]
    fetches = [
        pltpu.make_async_copy(src, dst, sem.at[0, i])
        for i, (src, dst) in enumerate(zip(ins, held))
    ]
    stores = [
        pltpu.make_async_copy(src, dst, sem.at[1, i])
        for i, (src, dst) in enumerate(zip(held, outs))
    ]
    for fetch in fetches:
        fetch.start()
    for fetch, store in zip(fetches, stores):
        fetch.wait()
        store.start()
    for store in stores:
        store.wait()


def per_device(
    nf,
    ny,
    features,
    weight,
    tile_bank,
    neighbors,
    tile_ids,
    edge_weight,
    counts,
    boundary,
    cotangent,
):
    nb = features.shape[2] // TILE
    per_pair = boundary.shape[2]
    nx = NX
    nz = nf // (2 * nx)
    chips = nf // 2
    half = chips * ROWS
    chunk = nf * ROWS // ny
    far = ny * ROWS
    lanes = NBANK * nb
    width = ROWS // GROUPS * TILE
    ring_rows = (nz - ZX) * nx * ROWS
    right = ny // 2
    left = ny - 1 - right
    scale = 1.0 / math.sqrt(ny * features.shape[2])
    hbm = pl.BlockSpec(memory_space=pl.ANY)
    dma = pltpu.SemaphoreType.DMA
    act, feature_grad, weight_grad = pl.pallas_call(
        functools.partial(kernel, nf, ny, per_pair, scale),
        out_shape=(
            jax.ShapeDtypeStruct((chips, 2, ROWS, TILE), BF16),
            jax.ShapeDtypeStruct((ROWS, nb * TILE), BF16),
            jax.ShapeDtypeStruct((ROWS, nf * ROWS), F32),
        ),
        in_specs=[hbm] * 9,
        out_specs=(hbm, hbm, hbm),
        scratch_shapes=[
            pltpu.VMEM((chips, 2, ROWS, TILE), BF16),
            pltpu.VMEM((ROWS, nb * TILE), BF16),
            pltpu.VMEM((ROWS, nf * ROWS), F32),
            pltpu.VMEM((per_pair, ny), jnp.int32),
            pltpu.VMEM((ROWS, nb * TILE), BF16),
            pltpu.VMEM((NBANK, TILE, TILE), BF16),
            pltpu.VMEM((K, nb), jnp.int32),
            pltpu.VMEM((K, nb), jnp.int32),
            pltpu.VMEM((K, nb), BF16),
            pltpu.VMEM((1, nb), jnp.int32),
            pltpu.VMEM((chips, 2, ROWS, TILE), BF16),
            pltpu.VMEM((nb * ROWS, TILE), F32),
            pltpu.VMEM((GROUPS, nb, width), BF16),
            pltpu.VMEM((ny, ROWS, width), BF16),
            pltpu.VMEM((ny, ROWS, width), BF16),
            pltpu.VMEM((GROUPS, lanes, width), F32),
            pltpu.VMEM((lanes, 2 * nb), BF16),
            pltpu.VMEM((GROUPS, lanes, 2 * far), BF16),
            pltpu.VMEM((2 * nb, lanes), BF16),
            pltpu.VMEM((2 * far, lanes), BF16),
            pltpu.VMEM((GROUPS, nb, far), BF16),
            pltpu.VMEM((TILE, NBANK * TILE), BF16),
            pltpu.VMEM((ROWS * nb, NBANK * TILE), BF16),
            pltpu.VMEM((nb, ROWS, TILE), BF16),
            pltpu.VMEM((nf, ROWS, TILE), BF16),
            pltpu.VMEM((nf, ROWS, TILE), BF16),
            pltpu.VMEM((2, nz, nx, ROWS, nf * ROWS), BF16),
            pltpu.VMEM((2, half, TILE), BF16),
            pltpu.VMEM((TILE, 2 * half), BF16),
            pltpu.VMEM((half, TILE), BF16),
            pltpu.VMEM((nf, ROWS, TILE), BF16),
            pltpu.VMEM((nf, ROWS, TILE), BF16),
            pltpu.VMEM((GROUPS, lanes, width), BF16),
            pltpu.VMEM((GROUPS, nb, width), F32),
            pltpu.VMEM((ny, ROWS, width), BF16),
            pltpu.VMEM((ny, ROWS, width), BF16),
            pltpu.VMEM((ny, nx, ZX, ROWS, chunk), BF16),
            pltpu.VMEM((ny, nx - 1, ZX, ROWS, chunk), BF16),
            pltpu.VMEM((ny, ZX, ROWS, chunk), BF16),
            pltpu.VMEM((nz * ny, ROWS, chunk), BF16),
            pltpu.VMEM((ny, ring_rows, chunk), F32),
            pltpu.VMEM((right, ring_rows, chunk), BF16),
            pltpu.VMEM((right, ring_rows, chunk), BF16),
            pltpu.VMEM((left, ring_rows, chunk), BF16),
            pltpu.VMEM((left, ring_rows, chunk), BF16),
            pltpu.VMEM(((nz - ZX) * nx, ROWS, chunk), BF16),
            pltpu.VMEM((chips, ROWS, chunk), BF16),
            pltpu.VMEM((ROWS, chunk), F32),
            pltpu.VMEM((ny, ROWS, chunk), F32),
            dma((12,)),
            pltpu.SemaphoreType.REGULAR,
            dma((9,)),
            dma((9,)),
            dma((nz,)),
            dma((nz,)),
            dma((nz,)),
            dma((nz,)),
            dma((nz,)),
            dma((nz,)),
            dma((ny,)),
            dma((ny,)),
            dma((2, right)),
            dma((2, right)),
        ],
        compiler_params=pltpu.CompilerParams(
            collective_id=0,
            has_side_effects=True,
            vmem_limit_bytes=60 * 2**20,
        ),
    )(
        boundary[:, 0, :].T,
        features[0],
        weight,
        tile_bank,
        neighbors[0].T,
        tile_ids[0].T,
        edge_weight[0].T,
        counts,
        cotangent[0].reshape(chips, 2, ROWS, TILE),
    )
    results = (act, feature_grad, weight_grad)
    act, feature_grad, weight_grad = pl.pallas_call(
        hand_over,
        out_shape=tuple(jax.ShapeDtypeStruct(a.shape, a.dtype) for a in results),
        in_specs=[hbm] * 3,
        out_specs=(hbm, hbm, hbm),
        scratch_shapes=[pltpu.VMEM(a.shape, a.dtype) for a in results]
        + [dma((2, 3))],
        compiler_params=pltpu.CompilerParams(vmem_limit_bytes=60 * 2**20),
    )(*results)
    return (
        act.reshape(cotangent.shape),
        feature_grad[None],
        weight_grad,
    )


def solution(mesh):
    in_specs = (
        P("dom", "feat", None),
        P("feat", None),
        P(),
        P("dom", None, None),
        P("dom", None, None),
        P("dom", None, None),
        P("dom", None),
        P(None, "dom", None),
        P("dom", None, "feat"),
    )
    out_specs = (P("dom", None, "feat"), P("dom", "feat", None), P("feat", None))
    return jax.shard_map(
        functools.partial(per_device, mesh.shape["feat"], mesh.shape["dom"]),
        mesh=mesh,
        in_specs=in_specs,
        out_specs=out_specs,
        check_vma=False,
    )
```

```python
import functools
import math

import jax
import jax.numpy as jnp
from jax import lax
from jax.experimental import pallas as pl
from jax.experimental.pallas import tpu as pltpu
from jax.sharding import PartitionSpec as P

TILE = 128
NBANK = 4
K = 8
ROWS = 16
GROUPS = 4
MESH = pl.DeviceIdType.MESH
F32 = jnp.float32
BF16 = jnp.bfloat16
NX = 4
EARLY = 3
MIDDLE = 5
ZX = 4

NT = (((1,), (1,)), ((), ()))


def dot(a, b):
    return jnp.dot(a, b, preferred_element_type=F32)


def kernel(
    nf,
    ny,
    per_pair,
    scale,
    bnd_hbm,
    x_hbm,
    w_hbm,
    bank_hbm,
    nbr_hbm,
    tid_hbm,
    ew_hbm,
    cnt_hbm,
    cot_hbm,
    act_hbm,
    fg_hbm,
    wg_hbm,
    act_ref,
    fg_ref,
    wg_ref,
    bnd_ref,
    x_ref,
    bank_ref,
    nbr_ref,
    tid_ref,
    ew_ref,
    cnt_ref,
    cot_ref,
    shuf,
    xk,
    out_blocks,
    land,
    near,
    an_bf,
    af_bf,
    atn_bf,
    atf_bf,
    oht_bf,
    bank_u,
    mixed,
    send_a,
    view,
    view2,
    wbuf,
    slope,
    slope_t,
    slope2,
    send_g,
    cols,
    back,
    own,
    send_d,
    land_d,
    send_x,
    land_x,
    send_z,
    land_z,
    rest_of,
    right_s,
    right_r,
    left_s,
    left_r,
    send_w,
    land_w,
    send_y,
    land_y,
    in_sem,
    go_sem,
    phase_s,
    phase_r,
    wz_s,
    wz_r,
    wx_s,
    wx_r,
    wp_s,
    wp_r,
    gx_s,
    gx_r,
    gr_s,
    gr_r,
):
    nb = nf
    nx = NX
    nz = nf // (2 * nx)
    chips = nf // 2
    chunk = nf * ROWS // ny
    per_chunk = chunk // ROWS
    half = chips * ROWS
    far = ny * ROWS
    lanes = NBANK * nb
    group = ROWS // GROUPS
    width = group * TILE
    zx = ZX
    zy = nz - zx
    ring_tiles = zy * nx
    ring_rows = ring_tiles * ROWS
    right = ny // 2
    left = ny - 1 - right

    me = lax.axis_index("feat")
    dom = lax.axis_index("dom")
    core = lax.rem(me, 2)
    col = lax.rem(lax.div(me, 2), nx)
    row = lax.div(me, 2 * nx)
    partner = me + 1 - 2 * core

    def device(z, x, c):
        return (z * nx + x) * 2 + c

    def at_dom(step):
        return lax.rem(dom + step + ny, ny)

    def at_row(step):
        return lax.rem(row + step + nz, nz)

    def at_col(step):
        return lax.rem(col + step + nx, nx)

    def copy_to(src, dst, send_sem, recv_sem, feat_id, dom_id):
        return pltpu.make_async_remote_copy(
            src_ref=src,
            dst_ref=dst,
            send_sem=send_sem,
            recv_sem=recv_sem,
            device_id=(feat_id, dom_id),
            device_id_type=MESH,
        )

    def wait_bytes(ref, sem):
        pltpu.make_async_copy(ref, ref, sem).wait()

    barrier = pltpu.get_barrier_semaphore()

    def greet(feat_id, dom_id):
        pl.semaphore_signal(
            barrier, inc=1, device_id=(feat_id, dom_id), device_id_type=MESH
        )

    for step in range(1, ny):
        greet(me, at_dom(step))
    for step in range(1, nz):
        greet(device(at_row(step), col, core), dom)
    for step in range(1, 2 * nx):
        greet(row * (2 * nx) + lax.rem(lax.rem(me, 2 * nx) + step, 2 * nx), dom)

    fetches = [
        pltpu.make_async_copy(src, dst, in_sem.at[i])
        for i, (src, dst) in enumerate(
            (
                (x_hbm, x_ref),
                (bnd_hbm, bnd_ref),
                (w_hbm, wbuf.at[core, row, col]),
                (nbr_hbm, nbr_ref),
                (tid_hbm, tid_ref),
                (ew_hbm, ew_ref),
                (cnt_hbm, cnt_ref),
                (bank_hbm, bank_ref),
                (cot_hbm, cot_ref),
            )
        )
    ]
    for fetch in fetches:
        fetch.start()
    for fetch in fetches[:3]:
        fetch.wait()

    for b in range(nb):
        shuf[b * ROWS : (b + 1) * ROWS, :] = x_ref[
            :, b * TILE : (b + 1) * TILE
        ].astype(F32)
    for f in range(ROWS):
        xk[f // group, :, (f % group) * TILE : (f % group + 1) * TILE] = shuf[
            pl.ds(f, nb, stride=ROWS), :
        ].astype(BF16)

    lane = lax.broadcasted_iota(jnp.int32, (per_pair, far), 1)
    spread = jnp.full((per_pair, far), -1, jnp.int32)
    for q in range(ny):
        spread = jnp.where(
            lax.div(lane, ROWS) == q, bnd_ref[:, q : q + 1], spread
        )
    lane = lax.broadcasted_iota(jnp.int32, (1, far), 1)
    lane_g = lax.rem(lax.div(lane, per_pair), GROUPS)
    lane_j = lax.rem(lane, per_pair)
    wanted = spread[0:1]
    for j in range(1, per_pair):
        wanted = jnp.where(lane_j == j, spread[j : j + 1], wanted)
    row_b = lax.broadcasted_iota(jnp.int32, (nb, far), 0)
    hots = [
        jnp.where((row_b == wanted) & (lane_g == g), 1.0, 0.0) for g in range(GROUPS)
    ]
    for g in range(GROUPS):
        oht_bf[g] = hots[g].astype(BF16)
    hot = jnp.concatenate(hots, axis=0).T.astype(BF16)
    out_blocks[...] = (
        dot(hot, xk[...].reshape(GROUPS * nb, width))
        .astype(BF16)
        .reshape(ny, ROWS, width)
    )

    pl.semaphore_wait(barrier, ny - 1 + nz - 1 + 2 * nx - 1)

    for step in range(1, nz):
        pl.semaphore_signal(
            go_sem,
            inc=1,
            device_id=(device(at_row(step), col, core), dom),
            device_id_type=MESH,
        )

    for step in range(1, ny):
        to = at_dom(step)
        copy_to(
            out_blocks.at[to], land.at[dom], phase_s.at[0], phase_r.at[0], me, to
        ).start()

    def weight_z(step):
        block = wbuf.at[core, row, col]
        return copy_to(
            block,
            block,
            wz_s.at[step],
            wz_r.at[step],
            device(at_row(step), col, core),
            dom,
        )

    def weight_x(step, aside):
        block = wbuf.at[core, at_row(-step), col]
        return copy_to(
            block,
            block,
            wx_s.at[step],
            wx_r.at[step],
            device(row, at_col(aside), core),
            dom,
        )

    def weight_pair(step):
        blocks = wbuf.at[core, at_row(-step)]
        return copy_to(blocks, blocks, wp_s.at[step], wp_r.at[step], partner, dom)

    order = [0]
    for step in range(1, nz // 2 + 1):
        order.append(step)
        if nz - step != step:
            order.append(nz - step)

    def forward_x(step):
        if step:
            wait_bytes(wbuf.at[core, at_row(-step), col], wz_r.at[step])
        for aside in range(1, nx):
            weight_x(step, aside).start()

    def forward_pair(step):
        wait_bytes(wbuf.at[core, at_row(-step), pl.ds(0, nx - 1)], wx_r.at[step])
        weight_pair(step).start()

    forward_x(0)
    for step in order[1:]:
        weight_z(step).start()
    land[dom] = out_blocks[dom]

    for fetch in fetches[3:]:
        fetch.wait()
    for t in range(NBANK):
        bank_u[:, t * TILE : (t + 1) * TILE] = bank_ref[t]
    nbr = jnp.concatenate([nbr_ref[...]] * NBANK, axis=1)
    tid = jnp.concatenate([tid_ref[...]] * NBANK, axis=1)
    edge = jnp.concatenate([ew_ref[...].astype(F32)] * NBANK, axis=1)
    cnt = jnp.concatenate([cnt_ref[...]] * NBANK, axis=1)
    lane_t = lax.div(lax.broadcasted_iota(jnp.int32, (K, lanes), 1), nb)
    slot = lax.broadcasted_iota(jnp.int32, (K, lanes), 0)
    coeff = jnp.where((tid == lane_t) & (slot < cnt), edge, 0.0)
    near_c = lax.broadcasted_iota(jnp.int32, (nb, lanes), 0)
    far_l = lax.broadcasted_iota(jnp.int32, (far, lanes), 0)
    far_c = nb + lax.div(far_l, ROWS) * per_pair + lax.rem(far_l, per_pair)
    at_near = jnp.zeros((nb, lanes), F32)
    at_far = jnp.zeros((far, lanes), F32)
    for k in range(K):
        at_near += jnp.where(near_c == nbr[k : k + 1], coeff[k : k + 1], 0.0)
        at_far += jnp.where(far_c == nbr[k : k + 1], coeff[k : k + 1], 0.0)
    near_hi = at_near.astype(BF16).astype(F32)
    far_hi = at_far.astype(BF16).astype(F32)
    near_2 = jnp.concatenate([near_hi, at_near - near_hi], axis=0)
    far_2 = jnp.concatenate([far_hi, at_far - far_hi], axis=0)
    atn_bf[...] = near_2.astype(BF16)
    atf_bf[...] = far_2.astype(BF16)
    an_bf[...] = near_2.T.astype(BF16)
    far_t = far_2.T
    lane_2 = lax.broadcasted_iota(jnp.int32, (lanes, 2 * far), 1)
    lane_2g = lax.rem(lax.div(lane_2, per_pair), GROUPS)
    for g in range(GROUPS):
        af_bf[g] = jnp.where(lane_2g == g, far_t, 0.0).astype(BF16)

    for g in range(GROUPS):
        near[g] = dot(an_bf[...], jnp.concatenate([xk[g]] * 2, axis=0))

    for step in order[1:EARLY]:
        forward_x(step)

    wait_bytes(land.at[pl.ds(0, ny - 1)], phase_r.at[0])
    landed = land[...].reshape(far, width)
    landed = jnp.concatenate([landed] * 2, axis=0)
    for g in range(GROUPS):
        mix = (near[g] + dot(af_bf[g], landed)).astype(BF16)
        for i in range(group):
            f = g * group + i
            for t in range(NBANK):
                mixed[f * nb : (f + 1) * nb, t * TILE : (t + 1) * TILE] = mix[
                    t * nb : (t + 1) * nb, i * TILE : (i + 1) * TILE
                ]
    for g in range(GROUPS):
        rows = group * nb
        agg = lax.dot_general(
            mixed[g * rows : (g + 1) * rows, :],
            bank_u[...],
            NT,
            preferred_element_type=F32,
        )
        for i in range(group):
            shuf[pl.ds(g * group + i, nb, stride=ROWS), :] = agg[i * nb : (i + 1) * nb]
    send_a[...] = shuf[...].astype(BF16).reshape(nb, ROWS, TILE)

    for step in order[EARLY:MIDDLE]:
        forward_x(step)
    pl.semaphore_wait(go_sem, nz - 1)

    def send_agg(step, carry):
        to = lax.rem(me + step, nf)
        copy_to(
            send_a.at[to], view.at[me], phase_s.at[1], phase_r.at[1], to, dom
        ).start()
        return carry

    lax.fori_loop(1, nf, send_agg, 0)
    view[me] = send_a[me]

    for step in order[MIDDLE:]:
        forward_x(step)
    for step in order:
        forward_pair(step)

    wait_bytes(view.at[pl.ds(0, nf - 1)], phase_r.at[1])
    view_copy = copy_to(view, view2, phase_s.at[2], phase_r.at[2], partner, dom)
    view_copy.start()

    rows_all = view[...].reshape(nf * ROWS, TILE)
    for turn in range(2):
        c = core if turn == 0 else 1 - core
        if turn == 1:
            for step in order:
                wait_bytes(wbuf.at[1 - core, at_row(-step)], wp_r.at[step])
        pre = dot(wbuf[c].reshape(half, nf * ROWS), rows_all)
        sig = jax.nn.sigmoid(pre)
        act_ref[:, c] = (pre * sig).astype(BF16).reshape(chips, ROWS, TILE)
        cot = cot_ref[:, c].reshape(half, TILE).astype(F32)
        slo = cot * (sig * (1.0 + pre * (1.0 - sig)))
        slo = slo.astype(BF16)
        slope[c] = slo

    slope_copy = copy_to(
        slope.at[1 - core], slope2, phase_s.at[3], phase_r.at[3], partner, dom
    )
    slope_copy.start()
    act_out = pltpu.make_async_copy(act_ref, act_hbm, in_sem.at[9])
    act_out.start()

    for c in range(2):
        slope_t[:, c * half : (c + 1) * half] = slope[c].astype(F32).T.astype(BF16)
    piece = 2 * chunk
    for s in range(0, ny, 2):
        at = slice(s * chunk, (s + 2) * chunk)
        lhs = jnp.concatenate(
            [wbuf[c, :, :, :, at].reshape(half, piece) for c in range(2)], axis=0
        )
        grad = dot(slope_t[...], lhs).T
        send_g[s * per_chunk : (s + 2) * per_chunk] = grad.astype(BF16).reshape(
            2 * per_chunk, ROWS, TILE
        )

    wait_bytes(view2, phase_r.at[2])
    wait_bytes(slope2, phase_r.at[3])
    own_slope = jnp.concatenate([slope[core], slope2[...]], axis=1)

    def partial_x(k, aside):
        to = at_col(aside)
        return copy_to(
            send_x.at[k, to],
            land_x.at[k, aside - 1],
            gx_s.at[k],
            gx_r.at[k],
            device(row, to, core),
            dom,
        )

    def send_grad(step, carry):
        to = lax.rem(me + step, nf)
        copy_to(
            send_g.at[to], cols.at[me], phase_s.at[4], phase_r.at[4], to, dom
        ).start()
        return carry

    lax.fori_loop(1, nf, send_grad, 0)
    cols[me] = send_g[me]

    def ring_copy(direction, k):
        src, dst = ((right_s, right_r), (left_s, left_r))[direction]
        return copy_to(
            src.at[k],
            dst.at[k],
            gr_s.at[direction, k],
            gr_r.at[direction, k],
            me,
            at_dom(1 - 2 * direction),
        )

    def to_columns(k):
        at = pl.ds(at_dom(k) * per_chunk, per_chunk)
        rhs = jnp.concatenate(
            [view[at].reshape(chunk, TILE), view2[at].reshape(chunk, TILE)], axis=1
        )
        part = lax.dot_general(own_slope, rhs, NT, preferred_element_type=F32)
        part = part.reshape(nz, nx, ROWS, chunk)
        for x in range(nx):
            send_x[k, x] = part[:zx, x].astype(BF16)
        for aside in range(1, nx):
            partial_x(k, aside).start()
        rest = part[zx:].reshape(ring_rows, chunk)
        if k == right:
            right_s[0] = rest.astype(BF16)
            ring_copy(0, 0).start()
        elif k == right + 1:
            left_s[0] = rest.astype(BF16)
            ring_copy(1, 0).start()
        else:
            rest_of[k] = rest

    near_far = [right, right + 1]
    for k in range(1, right):
        near_far.append(right - k)
        if right + 1 + k < ny:
            near_far.append(right + 1 + k)
    near_far.append(0)
    for k in near_far:
        to_columns(k)

    def ring_step(k):
        if k < right:
            wait_bytes(right_r.at[k - 1], gr_r.at[0, k - 1])
            right_s[k] = (rest_of[right - k] + right_r[k - 1].astype(F32)).astype(BF16)
            ring_copy(0, k).start()
        if k < left:
            wait_bytes(left_r.at[k - 1], gr_r.at[1, k - 1])
            left_s[k] = (
                rest_of[right + 1 + k] + left_r[k - 1].astype(F32)
            ).astype(BF16)
            ring_copy(1, k).start()

    def spread_out(k):
        to = at_dom(k)
        wait_bytes(land_x.at[k], gx_r.at[k])
        total = send_x[k, col].astype(F32)
        for aside in range(1, nx):
            total += land_x[k, aside - 1].astype(F32)
        send_z[k] = total.astype(BF16)
        for z in range(zx):
            tile = copy_to(
                send_z.at[k, z],
                land_z.at[row * ny + dom],
                phase_s.at[5],
                phase_r.at[5],
                device(z, col, core),
                to,
            )
            if k:
                tile.start()
            else:
                pl.when(row != z)(tile.start)

    ring_step(1)
    for k in near_far[:3]:
        spread_out(k)
    ring_step(2)
    for k in near_far[3:]:
        spread_out(k)

    wait_bytes(cols.at[pl.ds(0, nf - 1)], phase_r.at[4])
    shuf[...] = cols[...].reshape(nb * ROWS, TILE).astype(F32)
    for g in range(GROUPS):
        lhs = jnp.concatenate(
            [shuf[pl.ds(g * group + i, nb, stride=ROWS), :] for i in range(group)],
            axis=0,
        ).astype(BF16)
        mix = dot(lhs, bank_u[...]).astype(BF16)
        for i in range(group):
            for t in range(NBANK):
                back[g, t * nb : (t + 1) * nb, i * TILE : (i + 1) * TILE] = mix[
                    i * nb : (i + 1) * nb, t * TILE : (t + 1) * TILE
                ]
    far_rows = lax.broadcasted_iota(jnp.int32, (far, width), 0)
    far_g = lax.rem(lax.div(far_rows, per_pair), GROUPS)
    sent = jnp.zeros((far, width), F32)
    for g in range(GROUPS):
        both = dot(atf_bf[...], back[g])
        sent = jnp.where(far_g == g, both[:far] + both[far:], sent)
    send_d[...] = sent.astype(BF16).reshape(ny, ROWS, width)

    for step in range(1, ny):
        to = at_dom(step)
        copy_to(
            send_d.at[to], land_d.at[dom], phase_s.at[6], phase_r.at[6], me, to
        ).start()
    land_d[dom] = send_d[dom]

    if right > 1:
        ring_step(right - 1)

    @pl.when(row < zx)
    def _():
        land_z[row * ny + dom] = send_z[0, jnp.minimum(row, zx - 1)]

    for g in range(GROUPS):
        both = dot(atn_bf[...], back[g])
        own[g] = both[:nb] + both[nb:]

    wait_bytes(right_r.at[right - 1], gr_r.at[0, right - 1])
    wait_bytes(left_r.at[left - 1], gr_r.at[1, left - 1])
    send_w[...] = (
        (
            rest_of[0]
            + right_r[right - 1].astype(F32)
            + left_r[left - 1].astype(F32)
        )
        .astype(BF16)
        .reshape(ring_tiles, ROWS, chunk)
    )
    chip = row * nx + col
    for t in range(ring_tiles):
        z, x = zx + t // nx, t % nx
        tile = copy_to(
            send_w.at[t],
            land_w.at[chip],
            phase_s.at[8],
            phase_r.at[8],
            device(z, x, core),
            dom,
        )
        pl.when(chip != z * nx + x)(tile.start)

    @pl.when(row >= zx)
    def _():
        land_w[chip] = send_w[jnp.maximum(chip - zx * nx, 0)]

    wait_bytes(land_d.at[pl.ds(0, ny - 1)], phase_r.at[6])
    landed = land_d[...].reshape(far, width)
    for g in range(GROUPS):
        total = own[g] + dot(oht_bf[g], landed)
        for i in range(group):
            shuf[pl.ds(g * group + i, nb, stride=ROWS), :] = total[
                :, i * TILE : (i + 1) * TILE
            ]
    for b in range(nb):
        fg_ref[:, b * TILE : (b + 1) * TILE] = shuf[
            b * ROWS : (b + 1) * ROWS, :
        ].astype(BF16)

    fg_out = pltpu.make_async_copy(fg_ref, fg_hbm, in_sem.at[10])
    fg_out.start()

    @pl.when(row < zx)
    def _():
        wait_bytes(land_z.at[pl.ds(0, nz * ny - 1)], phase_r.at[5])
        rows_sum = land_z[0].astype(F32)
        for m in range(1, nz * ny):
            rows_sum += land_z[m].astype(F32)
        send_y[...] = rows_sum * scale

    @pl.when(row >= zx)
    def _():
        wait_bytes(land_w.at[pl.ds(0, chips - 1)], phase_r.at[8])
        rows_sum = land_w[0].astype(F32)
        for m in range(1, chips):
            rows_sum += land_w[m].astype(F32)
        send_y[...] = rows_sum * scale

    for step in range(1, ny):
        to = at_dom(step)
        copy_to(send_y, land_y.at[dom], phase_s.at[7], phase_r.at[7], me, to).start()
    land_y[dom] = send_y[...]

    wait_bytes(out_blocks.at[pl.ds(0, ny - 1)], phase_s.at[0])
    wait_bytes(send_a.at[pl.ds(0, nf - 1)], phase_s.at[1])
    view_copy.wait_send()
    slope_copy.wait_send()
    wait_bytes(send_g.at[pl.ds(0, nf - 1)], phase_s.at[4])
    @pl.when(row < zx)
    def _():
        wait_bytes(land_z.at[pl.ds(0, zx * ny - 1)], phase_s.at[5])
        wait_bytes(land_w.at[pl.ds(0, ring_tiles)], phase_s.at[8])

    @pl.when(row >= zx)
    def _():
        wait_bytes(land_z.at[pl.ds(0, zx * ny)], phase_s.at[5])
        wait_bytes(land_w.at[pl.ds(0, ring_tiles - 1)], phase_s.at[8])

    for k in range(right):
        ring_copy(0, k).wait_send()
    for k in range(left):
        ring_copy(1, k).wait_send()
    wait_bytes(send_d.at[pl.ds(0, ny - 1)], phase_s.at[6])
    for step in order:
        if step:
            weight_z(step).wait_send()
        wait_bytes(wbuf.at[0, 0, pl.ds(0, nx - 1)], wx_s.at[step])
        weight_pair(step).wait_send()
    for k in range(ny):
        wait_bytes(land_x.at[k], gx_s.at[k])

    wait_bytes(land_y.at[pl.ds(0, ny - 1)], phase_r.at[7])
    for s in range(ny):
        wg_ref[:, s * chunk : (s + 1) * chunk] = land_y[s]
    wg_out = pltpu.make_async_copy(wg_ref, wg_hbm, in_sem.at[11])
    wg_out.start()
    act_out.wait()
    fg_out.wait()
    wg_out.wait()
    wait_bytes(land_y.at[pl.ds(0, ny - 1)], phase_s.at[7])


def hand_over(*refs):
    n = len(refs) // 3
    ins, outs, held, sem = refs[:n], refs[n : 2 * n], refs[2 * n : 3 * n], refs[-1]
    fetches = [
        pltpu.make_async_copy(src, dst, sem.at[0, i])
        for i, (src, dst) in enumerate(zip(ins, held))
    ]
    stores = [
        pltpu.make_async_copy(src, dst, sem.at[1, i])
        for i, (src, dst) in enumerate(zip(held, outs))
    ]
    for fetch in fetches:
        fetch.start()
    for fetch, store in zip(fetches, stores):
        fetch.wait()
        store.start()
    for store in stores:
        store.wait()


def per_device(
    nf,
    ny,
    features,
    weight,
    tile_bank,
    neighbors,
    tile_ids,
    edge_weight,
    counts,
    boundary,
    cotangent,
):
    nb = features.shape[2] // TILE
    per_pair = boundary.shape[2]
    nx = NX
    nz = nf // (2 * nx)
    chips = nf // 2
    half = chips * ROWS
    chunk = nf * ROWS // ny
    far = ny * ROWS
    lanes = NBANK * nb
    width = ROWS // GROUPS * TILE
    ring_rows = (nz - ZX) * nx * ROWS
    right = ny // 2
    left = ny - 1 - right
    scale = 1.0 / math.sqrt(ny * features.shape[2])
    hbm = pl.BlockSpec(memory_space=pl.ANY)
    dma = pltpu.SemaphoreType.DMA
    act, feature_grad, weight_grad = pl.pallas_call(
        functools.partial(kernel, nf, ny, per_pair, scale),
        out_shape=(
            jax.ShapeDtypeStruct((chips, 2, ROWS, TILE), BF16),
            jax.ShapeDtypeStruct((ROWS, nb * TILE), BF16),
            jax.ShapeDtypeStruct((ROWS, nf * ROWS), F32),
        ),
        in_specs=[hbm] * 9,
        out_specs=(hbm, hbm, hbm),
        scratch_shapes=[
            pltpu.VMEM((chips, 2, ROWS, TILE), BF16),
            pltpu.VMEM((ROWS, nb * TILE), BF16),
            pltpu.VMEM((ROWS, nf * ROWS), F32),
            pltpu.VMEM((per_pair, ny), jnp.int32),
            pltpu.VMEM((ROWS, nb * TILE), BF16),
            pltpu.VMEM((NBANK, TILE, TILE), BF16),
            pltpu.VMEM((K, nb), jnp.int32),
            pltpu.VMEM((K, nb), jnp.int32),
            pltpu.VMEM((K, nb), BF16),
            pltpu.VMEM((1, nb), jnp.int32),
            pltpu.VMEM((chips, 2, ROWS, TILE), BF16),
            pltpu.VMEM((nb * ROWS, TILE), F32),
            pltpu.VMEM((GROUPS, nb, width), BF16),
            pltpu.VMEM((ny, ROWS, width), BF16),
            pltpu.VMEM((ny, ROWS, width), BF16),
            pltpu.VMEM((GROUPS, lanes, width), F32),
            pltpu.VMEM((lanes, 2 * nb), BF16),
            pltpu.VMEM((GROUPS, lanes, 2 * far), BF16),
            pltpu.VMEM((2 * nb, lanes), BF16),
            pltpu.VMEM((2 * far, lanes), BF16),
            pltpu.VMEM((GROUPS, nb, far), BF16),
            pltpu.VMEM((TILE, NBANK * TILE), BF16),
            pltpu.VMEM((ROWS * nb, NBANK * TILE), BF16),
            pltpu.VMEM((nb, ROWS, TILE), BF16),
            pltpu.VMEM((nf, ROWS, TILE), BF16),
            pltpu.VMEM((nf, ROWS, TILE), BF16),
            pltpu.VMEM((2, nz, nx, ROWS, nf * ROWS), BF16),
            pltpu.VMEM((2, half, TILE), BF16),
            pltpu.VMEM((TILE, 2 * half), BF16),
            pltpu.VMEM((half, TILE), BF16),
            pltpu.VMEM((nf, ROWS, TILE), BF16),
            pltpu.VMEM((nf, ROWS, TILE), BF16),
            pltpu.VMEM((GROUPS, lanes, width), BF16),
            pltpu.VMEM((GROUPS, nb, width), F32),
            pltpu.VMEM((ny, ROWS, width), BF16),
            pltpu.VMEM((ny, ROWS, width), BF16),
            pltpu.VMEM((ny, nx, ZX, ROWS, chunk), BF16),
            pltpu.VMEM((ny, nx - 1, ZX, ROWS, chunk), BF16),
            pltpu.VMEM((ny, ZX, ROWS, chunk), BF16),
            pltpu.VMEM((nz * ny, ROWS, chunk), BF16),
            pltpu.VMEM((ny, ring_rows, chunk), F32),
            pltpu.VMEM((right, ring_rows, chunk), BF16),
            pltpu.VMEM((right, ring_rows, chunk), BF16),
            pltpu.VMEM((left, ring_rows, chunk), BF16),
            pltpu.VMEM((left, ring_rows, chunk), BF16),
            pltpu.VMEM(((nz - ZX) * nx, ROWS, chunk), BF16),
            pltpu.VMEM((chips, ROWS, chunk), BF16),
            pltpu.VMEM((ROWS, chunk), F32),
            pltpu.VMEM((ny, ROWS, chunk), F32),
            dma((12,)),
            pltpu.SemaphoreType.REGULAR,
            dma((9,)),
            dma((9,)),
            dma((nz,)),
            dma((nz,)),
            dma((nz,)),
            dma((nz,)),
            dma((nz,)),
            dma((nz,)),
            dma((ny,)),
            dma((ny,)),
            dma((2, right)),
            dma((2, right)),
        ],
        compiler_params=pltpu.CompilerParams(
            collective_id=0,
            has_side_effects=True,
            vmem_limit_bytes=60 * 2**20,
        ),
    )(
        boundary[:, 0, :].T,
        features[0],
        weight,
        tile_bank,
        neighbors[0].T,
        tile_ids[0].T,
        edge_weight[0].T,
        counts,
        cotangent[0].reshape(chips, 2, ROWS, TILE),
    )
    results = (act, feature_grad, weight_grad)
    act, feature_grad, weight_grad = pl.pallas_call(
        hand_over,
        out_shape=tuple(jax.ShapeDtypeStruct(a.shape, a.dtype) for a in results),
        in_specs=[hbm] * 3,
        out_specs=(hbm, hbm, hbm),
        scratch_shapes=[pltpu.VMEM(a.shape, a.dtype) for a in results]
        + [dma((2, 3))],
        compiler_params=pltpu.CompilerParams(vmem_limit_bytes=60 * 2**20),
    )(*results)
    return (
        act.reshape(cotangent.shape),
        feature_grad[None],
        weight_grad,
    )


def solution(mesh):
    in_specs = (
        P("dom", "feat", None),
        P("feat", None),
        P(),
        P("dom", None, None),
        P("dom", None, None),
        P("dom", None, None),
        P("dom", None),
        P(None, "dom", None),
        P("dom", None, "feat"),
    )
    out_specs = (P("dom", None, "feat"), P("dom", "feat", None), P("feat", None))
    return jax.shard_map(
        functools.partial(per_device, mesh.shape["feat"], mesh.shape["dom"]),
        mesh=mesh,
        in_specs=in_specs,
        out_specs=out_specs,
        check_vma=False,
    )
```

```python
import functools
import math

import jax
import jax.numpy as jnp
from jax import lax
from jax.experimental import pallas as pl
from jax.experimental.pallas import tpu as pltpu
from jax.sharding import PartitionSpec as P

TILE = 128
NBANK = 4
K = 8
ROWS = 16
GROUPS = 4
MESH = pl.DeviceIdType.MESH
F32 = jnp.float32
BF16 = jnp.bfloat16
NX = 4
EARLY = 5
MIDDLE = 5
ZX = 4

NT = (((1,), (1,)), ((), ()))


def dot(a, b):
    return jnp.dot(a, b, preferred_element_type=F32)


def kernel(
    nf,
    ny,
    per_pair,
    scale,
    bnd_hbm,
    x_hbm,
    w_hbm,
    bank_hbm,
    nbr_hbm,
    tid_hbm,
    ew_hbm,
    cnt_hbm,
    cot_hbm,
    act_hbm,
    fg_hbm,
    wg_hbm,
    act_ref,
    fg_ref,
    wg_ref,
    bnd_ref,
    x_ref,
    bank_ref,
    nbr_ref,
    tid_ref,
    ew_ref,
    cnt_ref,
    cot_ref,
    shuf,
    xk,
    out_blocks,
    land,
    near,
    an_bf,
    af_bf,
    atn_bf,
    atf_bf,
    oht_bf,
    bank_u,
    mixed,
    send_a,
    view,
    view2,
    wbuf,
    slope,
    slope_t,
    slope2,
    send_g,
    cols,
    back,
    own,
    send_d,
    land_d,
    send_x,
    land_x,
    send_z,
    land_z,
    rest_of,
    right_s,
    right_r,
    left_s,
    left_r,
    send_w,
    land_w,
    send_y,
    land_y,
    in_sem,
    go_sem,
    phase_s,
    phase_r,
    wz_s,
    wz_r,
    wx_s,
    wx_r,
    wp_s,
    wp_r,
    gx_s,
    gx_r,
    gr_s,
    gr_r,
):
    nb = nf
    nx = NX
    nz = nf // (2 * nx)
    chips = nf // 2
    chunk = nf * ROWS // ny
    per_chunk = chunk // ROWS
    half = chips * ROWS
    far = ny * ROWS
    lanes = NBANK * nb
    group = ROWS // GROUPS
    width = group * TILE
    zx = ZX
    zy = nz - zx
    ring_tiles = zy * nx
    ring_rows = ring_tiles * ROWS
    right = ny // 2
    left = ny - 1 - right

    me = lax.axis_index("feat")
    dom = lax.axis_index("dom")
    core = lax.rem(me, 2)
    col = lax.rem(lax.div(me, 2), nx)
    row = lax.div(me, 2 * nx)
    partner = me + 1 - 2 * core

    def device(z, x, c):
        return (z * nx + x) * 2 + c

    def at_dom(step):
        return lax.rem(dom + step + ny, ny)

    def at_row(step):
        return lax.rem(row + step + nz, nz)

    def at_col(step):
        return lax.rem(col + step + nx, nx)

    def copy_to(src, dst, send_sem, recv_sem, feat_id, dom_id):
        return pltpu.make_async_remote_copy(
            src_ref=src,
            dst_ref=dst,
            send_sem=send_sem,
            recv_sem=recv_sem,
            device_id=(feat_id, dom_id),
            device_id_type=MESH,
        )

    def wait_bytes(ref, sem):
        pltpu.make_async_copy(ref, ref, sem).wait()

    barrier = pltpu.get_barrier_semaphore()

    def greet(feat_id, dom_id):
        pl.semaphore_signal(
            barrier, inc=1, device_id=(feat_id, dom_id), device_id_type=MESH
        )

    for step in range(1, ny):
        greet(me, at_dom(step))
    for step in range(1, nz):
        greet(device(at_row(step), col, core), dom)
    for step in range(1, 2 * nx):
        greet(row * (2 * nx) + lax.rem(lax.rem(me, 2 * nx) + step, 2 * nx), dom)

    fetches = [
        pltpu.make_async_copy(src, dst, in_sem.at[i])
        for i, (src, dst) in enumerate(
            (
                (x_hbm, x_ref),
                (bnd_hbm, bnd_ref),
                (w_hbm, wbuf.at[core, row, col]),
                (nbr_hbm, nbr_ref),
                (tid_hbm, tid_ref),
                (ew_hbm, ew_ref),
                (cnt_hbm, cnt_ref),
                (bank_hbm, bank_ref),
                (cot_hbm, cot_ref),
            )
        )
    ]
    for fetch in fetches:
        fetch.start()
    for fetch in fetches[:3]:
        fetch.wait()

    for b in range(nb):
        shuf[b * ROWS : (b + 1) * ROWS, :] = x_ref[
            :, b * TILE : (b + 1) * TILE
        ].astype(F32)
    for f in range(ROWS):
        xk[f // group, :, (f % group) * TILE : (f % group + 1) * TILE] = shuf[
            pl.ds(f, nb, stride=ROWS), :
        ].astype(BF16)

    lane = lax.broadcasted_iota(jnp.int32, (per_pair, far), 1)
    spread = jnp.full((per_pair, far), -1, jnp.int32)
    for q in range(ny):
        spread = jnp.where(
            lax.div(lane, ROWS) == q, bnd_ref[:, q : q + 1], spread
        )
    lane = lax.broadcasted_iota(jnp.int32, (1, far), 1)
    lane_g = lax.rem(lax.div(lane, per_pair), GROUPS)
    lane_j = lax.rem(lane, per_pair)
    wanted = spread[0:1]
    for j in range(1, per_pair):
        wanted = jnp.where(lane_j == j, spread[j : j + 1], wanted)
    row_b = lax.broadcasted_iota(jnp.int32, (nb, far), 0)
    hots = [
        jnp.where((row_b == wanted) & (lane_g == g), 1.0, 0.0) for g in range(GROUPS)
    ]
    for g in range(GROUPS):
        oht_bf[g] = hots[g].astype(BF16)
    hot = jnp.concatenate(hots, axis=0).T.astype(BF16)
    out_blocks[...] = (
        dot(hot, xk[...].reshape(GROUPS * nb, width))
        .astype(BF16)
        .reshape(ny, ROWS, width)
    )

    pl.semaphore_wait(barrier, ny - 1 + nz - 1 + 2 * nx - 1)

    for step in range(1, nz):
        pl.semaphore_signal(
            go_sem,
            inc=1,
            device_id=(device(at_row(step), col, core), dom),
            device_id_type=MESH,
        )

    for step in range(1, ny):
        to = at_dom(step)
        copy_to(
            out_blocks.at[to], land.at[dom], phase_s.at[0], phase_r.at[0], me, to
        ).start()

    def weight_z(step):
        block = wbuf.at[core, row, col]
        return copy_to(
            block,
            block,
            wz_s.at[step],
            wz_r.at[step],
            device(at_row(step), col, core),
            dom,
        )

    def weight_x(step, aside):
        block = wbuf.at[core, at_row(-step), col]
        return copy_to(
            block,
            block,
            wx_s.at[step],
            wx_r.at[step],
            device(row, at_col(aside), core),
            dom,
        )

    def weight_pair(step):
        blocks = wbuf.at[core, at_row(-step)]
        return copy_to(blocks, blocks, wp_s.at[step], wp_r.at[step], partner, dom)

    order = [0]
    for step in range(1, nz // 2 + 1):
        order.append(step)
        if nz - step != step:
            order.append(nz - step)

    def forward_x(step):
        if step:
            wait_bytes(wbuf.at[core, at_row(-step), col], wz_r.at[step])
        for aside in range(1, nx):
            weight_x(step, aside).start()

    def forward_pair(step):
        wait_bytes(wbuf.at[core, at_row(-step), pl.ds(0, nx - 1)], wx_r.at[step])
        weight_pair(step).start()

    forward_x(0)
    for step in order[1:]:
        weight_z(step).start()
    land[dom] = out_blocks[dom]

    for fetch in fetches[3:]:
        fetch.wait()
    for t in range(NBANK):
        bank_u[:, t * TILE : (t + 1) * TILE] = bank_ref[t]
    nbr = jnp.concatenate([nbr_ref[...]] * NBANK, axis=1)
    tid = jnp.concatenate([tid_ref[...]] * NBANK, axis=1)
    edge = jnp.concatenate([ew_ref[...].astype(F32)] * NBANK, axis=1)
    cnt = jnp.concatenate([cnt_ref[...]] * NBANK, axis=1)
    lane_t = lax.div(lax.broadcasted_iota(jnp.int32, (K, lanes), 1), nb)
    slot = lax.broadcasted_iota(jnp.int32, (K, lanes), 0)
    coeff = jnp.where((tid == lane_t) & (slot < cnt), edge, 0.0)
    near_c = lax.broadcasted_iota(jnp.int32, (nb, lanes), 0)
    far_l = lax.broadcasted_iota(jnp.int32, (far, lanes), 0)
    far_c = nb + lax.div(far_l, ROWS) * per_pair + lax.rem(far_l, per_pair)
    at_near = jnp.zeros((nb, lanes), F32)
    at_far = jnp.zeros((far, lanes), F32)
    for k in range(K):
        at_near += jnp.where(near_c == nbr[k : k + 1], coeff[k : k + 1], 0.0)
        at_far += jnp.where(far_c == nbr[k : k + 1], coeff[k : k + 1], 0.0)
    near_hi = at_near.astype(BF16).astype(F32)
    far_hi = at_far.astype(BF16).astype(F32)
    near_2 = jnp.concatenate([near_hi, at_near - near_hi], axis=0)
    far_2 = jnp.concatenate([far_hi, at_far - far_hi], axis=0)
    atn_bf[...] = near_2.astype(BF16)
    atf_bf[...] = far_2.astype(BF16)
    an_bf[...] = near_2.T.astype(BF16)
    far_t = far_2.T
    lane_2 = lax.broadcasted_iota(jnp.int32, (lanes, 2 * far), 1)
    lane_2g = lax.rem(lax.div(lane_2, per_pair), GROUPS)
    for g in range(GROUPS):
        af_bf[g] = jnp.where(lane_2g == g, far_t, 0.0).astype(BF16)

    for g in range(GROUPS):
        near[g] = dot(an_bf[...], jnp.concatenate([xk[g]] * 2, axis=0))

    for step in order[1:EARLY]:
        forward_x(step)

    wait_bytes(land.at[pl.ds(0, ny - 1)], phase_r.at[0])
    landed = land[...].reshape(far, width)
    landed = jnp.concatenate([landed] * 2, axis=0)
    for g in range(GROUPS):
        mix = (near[g] + dot(af_bf[g], landed)).astype(BF16)
        for i in range(group):
            f = g * group + i
            for t in range(NBANK):
                mixed[f * nb : (f + 1) * nb, t * TILE : (t + 1) * TILE] = mix[
                    t * nb : (t + 1) * nb, i * TILE : (i + 1) * TILE
                ]
    for g in range(GROUPS):
        rows = group * nb
        agg = lax.dot_general(
            mixed[g * rows : (g + 1) * rows, :],
            bank_u[...],
            NT,
            preferred_element_type=F32,
        )
        for i in range(group):
            shuf[pl.ds(g * group + i, nb, stride=ROWS), :] = agg[i * nb : (i + 1) * nb]
    send_a[...] = shuf[...].astype(BF16).reshape(nb, ROWS, TILE)

    for step in order[EARLY:MIDDLE]:
        forward_x(step)
    pl.semaphore_wait(go_sem, nz - 1)

    def send_agg(step, carry):
        to = lax.rem(me + step, nf)
        copy_to(
            send_a.at[to], view.at[me], phase_s.at[1], phase_r.at[1], to, dom
        ).start()
        return carry

    lax.fori_loop(1, nf, send_agg, 0)
    view[me] = send_a[me]

    for step in order[MIDDLE:]:
        forward_x(step)
    for step in order:
        forward_pair(step)

    wait_bytes(view.at[pl.ds(0, nf - 1)], phase_r.at[1])
    view_copy = copy_to(view, view2, phase_s.at[2], phase_r.at[2], partner, dom)
    view_copy.start()

    rows_all = view[...].reshape(nf * ROWS, TILE)
    for turn in range(2):
        c = core if turn == 0 else 1 - core
        if turn == 1:
            for step in order:
                wait_bytes(wbuf.at[1 - core, at_row(-step)], wp_r.at[step])
        pre = dot(wbuf[c].reshape(half, nf * ROWS), rows_all)
        sig = jax.nn.sigmoid(pre)
        act_ref[:, c] = (pre * sig).astype(BF16).reshape(chips, ROWS, TILE)
        cot = cot_ref[:, c].reshape(half, TILE).astype(F32)
        slo = cot * (sig * (1.0 + pre * (1.0 - sig)))
        slo = slo.astype(BF16)
        slope[c] = slo

    slope_copy = copy_to(
        slope.at[1 - core], slope2, phase_s.at[3], phase_r.at[3], partner, dom
    )
    slope_copy.start()
    act_out = pltpu.make_async_copy(act_ref, act_hbm, in_sem.at[9])
    act_out.start()

    for c in range(2):
        slope_t[:, c * half : (c + 1) * half] = slope[c].astype(F32).T.astype(BF16)
    piece = 2 * chunk
    for s in range(0, ny, 2):
        at = slice(s * chunk, (s + 2) * chunk)
        lhs = jnp.concatenate(
            [wbuf[c, :, :, :, at].reshape(half, piece) for c in range(2)], axis=0
        )
        grad = dot(slope_t[...], lhs).T
        send_g[s * per_chunk : (s + 2) * per_chunk] = grad.astype(BF16).reshape(
            2 * per_chunk, ROWS, TILE
        )

    wait_bytes(view2, phase_r.at[2])
    wait_bytes(slope2, phase_r.at[3])
    own_slope = jnp.concatenate([slope[core], slope2[...]], axis=1)

    def partial_x(k, aside):
        to = at_col(aside)
        return copy_to(
            send_x.at[k, to],
            land_x.at[k, aside - 1],
            gx_s.at[k],
            gx_r.at[k],
            device(row, to, core),
            dom,
        )

    def send_grad(step, carry):
        to = lax.rem(me + step, nf)
        copy_to(
            send_g.at[to], cols.at[me], phase_s.at[4], phase_r.at[4], to, dom
        ).start()
        return carry

    lax.fori_loop(1, nf, send_grad, 0)
    cols[me] = send_g[me]

    def ring_copy(direction, k):
        src, dst = ((right_s, right_r), (left_s, left_r))[direction]
        return copy_to(
            src.at[k],
            dst.at[k],
            gr_s.at[direction, k],
            gr_r.at[direction, k],
            me,
            at_dom(1 - 2 * direction),
        )

    def to_columns(k):
        at = pl.ds(at_dom(k) * per_chunk, per_chunk)
        rhs = jnp.concatenate(
            [view[at].reshape(chunk, TILE), view2[at].reshape(chunk, TILE)], axis=1
        )
        part = lax.dot_general(own_slope, rhs, NT, preferred_element_type=F32)
        part = part.reshape(nz, nx, ROWS, chunk)
        for x in range(nx):
            send_x[k, x] = part[:zx, x].astype(BF16)
        for aside in range(1, nx):
            partial_x(k, aside).start()
        rest = part[zx:].reshape(ring_rows, chunk)
        if k == right:
            right_s[0] = rest.astype(BF16)
            ring_copy(0, 0).start()
        elif k == right + 1:
            left_s[0] = rest.astype(BF16)
            ring_copy(1, 0).start()
        else:
            rest_of[k] = rest

    near_far = [right, right + 1]
    for k in range(1, right):
        near_far.append(right - k)
        if right + 1 + k < ny:
            near_far.append(right + 1 + k)
    near_far.append(0)
    for k in near_far:
        to_columns(k)

    def ring_step(k):
        if k < right:
            wait_bytes(right_r.at[k - 1], gr_r.at[0, k - 1])
            right_s[k] = (rest_of[right - k] + right_r[k - 1].astype(F32)).astype(BF16)
            ring_copy(0, k).start()
        if k < left:
            wait_bytes(left_r.at[k - 1], gr_r.at[1, k - 1])
            left_s[k] = (
                rest_of[right + 1 + k] + left_r[k - 1].astype(F32)
            ).astype(BF16)
            ring_copy(1, k).start()

    def spread_out(k):
        to = at_dom(k)
        wait_bytes(land_x.at[k], gx_r.at[k])
        total = send_x[k, col].astype(F32)
        for aside in range(1, nx):
            total += land_x[k, aside - 1].astype(F32)
        send_z[k] = total.astype(BF16)
        for z in range(zx):
            tile = copy_to(
                send_z.at[k, z],
                land_z.at[row * ny + dom],
                phase_s.at[5],
                phase_r.at[5],
                device(z, col, core),
                to,
            )
            if k:
                tile.start()
            else:
                pl.when(row != z)(tile.start)

    ring_step(1)
    for k in near_far[:3]:
        spread_out(k)
    ring_step(2)
    for k in near_far[3:]:
        spread_out(k)

    wait_bytes(cols.at[pl.ds(0, nf - 1)], phase_r.at[4])
    shuf[...] = cols[...].reshape(nb * ROWS, TILE).astype(F32)
    for g in range(GROUPS):
        lhs = jnp.concatenate(
            [shuf[pl.ds(g * group + i, nb, stride=ROWS), :] for i in range(group)],
            axis=0,
        ).astype(BF16)
        mix = dot(lhs, bank_u[...]).astype(BF16)
        for i in range(group):
            for t in range(NBANK):
                back[g, t * nb : (t + 1) * nb, i * TILE : (i + 1) * TILE] = mix[
                    i * nb : (i + 1) * nb, t * TILE : (t + 1) * TILE
                ]
    far_rows = lax.broadcasted_iota(jnp.int32, (far, width), 0)
    far_g = lax.rem(lax.div(far_rows, per_pair), GROUPS)
    sent = jnp.zeros((far, width), F32)
    for g in range(GROUPS):
        both = dot(atf_bf[...], back[g])
        sent = jnp.where(far_g == g, both[:far] + both[far:], sent)
    send_d[...] = sent.astype(BF16).reshape(ny, ROWS, width)

    for step in range(1, ny):
        to = at_dom(step)
        copy_to(
            send_d.at[to], land_d.at[dom], phase_s.at[6], phase_r.at[6], me, to
        ).start()
    land_d[dom] = send_d[dom]

    if right > 1:
        ring_step(right - 1)

    @pl.when(row < zx)
    def _():
        land_z[row * ny + dom] = send_z[0, jnp.minimum(row, zx - 1)]

    for g in range(GROUPS):
        both = dot(atn_bf[...], back[g])
        own[g] = both[:nb] + both[nb:]

    wait_bytes(right_r.at[right - 1], gr_r.at[0, right - 1])
    wait_bytes(left_r.at[left - 1], gr_r.at[1, left - 1])
    send_w[...] = (
        (
            rest_of[0]
            + right_r[right - 1].astype(F32)
            + left_r[left - 1].astype(F32)
        )
        .astype(BF16)
        .reshape(ring_tiles, ROWS, chunk)
    )
    chip = row * nx + col
    for t in range(ring_tiles):
        z, x = zx + t // nx, t % nx
        tile = copy_to(
            send_w.at[t],
            land_w.at[chip],
            phase_s.at[8],
            phase_r.at[8],
            device(z, x, core),
            dom,
        )
        pl.when(chip != z * nx + x)(tile.start)

    @pl.when(row >= zx)
    def _():
        land_w[chip] = send_w[jnp.maximum(chip - zx * nx, 0)]

    wait_bytes(land_d.at[pl.ds(0, ny - 1)], phase_r.at[6])
    landed = land_d[...].reshape(far, width)
    for g in range(GROUPS):
        total = own[g] + dot(oht_bf[g], landed)
        for i in range(group):
            shuf[pl.ds(g * group + i, nb, stride=ROWS), :] = total[
                :, i * TILE : (i + 1) * TILE
            ]
    for b in range(nb):
        fg_ref[:, b * TILE : (b + 1) * TILE] = shuf[
            b * ROWS : (b + 1) * ROWS, :
        ].astype(BF16)

    fg_out = pltpu.make_async_copy(fg_ref, fg_hbm, in_sem.at[10])
    fg_out.start()

    @pl.when(row < zx)
    def _():
        wait_bytes(land_z.at[pl.ds(0, nz * ny - 1)], phase_r.at[5])
        rows_sum = land_z[0].astype(F32)
        for m in range(1, nz * ny):
            rows_sum += land_z[m].astype(F32)
        send_y[...] = rows_sum * scale

    @pl.when(row >= zx)
    def _():
        wait_bytes(land_w.at[pl.ds(0, chips - 1)], phase_r.at[8])
        rows_sum = land_w[0].astype(F32)
        for m in range(1, chips):
            rows_sum += land_w[m].astype(F32)
        send_y[...] = rows_sum * scale

    for step in range(1, ny):
        to = at_dom(step)
        copy_to(send_y, land_y.at[dom], phase_s.at[7], phase_r.at[7], me, to).start()
    land_y[dom] = send_y[...]

    wait_bytes(out_blocks.at[pl.ds(0, ny - 1)], phase_s.at[0])
    wait_bytes(send_a.at[pl.ds(0, nf - 1)], phase_s.at[1])
    view_copy.wait_send()
    slope_copy.wait_send()
    wait_bytes(send_g.at[pl.ds(0, nf - 1)], phase_s.at[4])
    @pl.when(row < zx)
    def _():
        wait_bytes(land_z.at[pl.ds(0, zx * ny - 1)], phase_s.at[5])
        wait_bytes(land_w.at[pl.ds(0, ring_tiles)], phase_s.at[8])

    @pl.when(row >= zx)
    def _():
        wait_bytes(land_z.at[pl.ds(0, zx * ny)], phase_s.at[5])
        wait_bytes(land_w.at[pl.ds(0, ring_tiles - 1)], phase_s.at[8])

    for k in range(right):
        ring_copy(0, k).wait_send()
    for k in range(left):
        ring_copy(1, k).wait_send()
    wait_bytes(send_d.at[pl.ds(0, ny - 1)], phase_s.at[6])
    for step in order:
        if step:
            weight_z(step).wait_send()
        wait_bytes(wbuf.at[0, 0, pl.ds(0, nx - 1)], wx_s.at[step])
        weight_pair(step).wait_send()
    for k in range(ny):
        wait_bytes(land_x.at[k], gx_s.at[k])

    wait_bytes(land_y.at[pl.ds(0, ny - 1)], phase_r.at[7])
    for s in range(ny):
        wg_ref[:, s * chunk : (s + 1) * chunk] = land_y[s]
    wg_out = pltpu.make_async_copy(wg_ref, wg_hbm, in_sem.at[11])
    wg_out.start()
    act_out.wait()
    fg_out.wait()
    wg_out.wait()
    wait_bytes(land_y.at[pl.ds(0, ny - 1)], phase_s.at[7])


def hand_over(*refs):
    n = len(refs) // 3
    ins, outs, held, sem = refs[:n], refs[n : 2 * n], refs[2 * n : 3 * n], refs[-1]
    fetches = [
        pltpu.make_async_copy(src, dst, sem.at[0, i])
        for i, (src, dst) in enumerate(zip(ins, held))
    ]
    stores = [
        pltpu.make_async_copy(src, dst, sem.at[1, i])
        for i, (src, dst) in enumerate(zip(held, outs))
    ]
    for fetch in fetches:
        fetch.start()
    for fetch, store in zip(fetches, stores):
        fetch.wait()
        store.start()
    for store in stores:
        store.wait()


def per_device(
    nf,
    ny,
    features,
    weight,
    tile_bank,
    neighbors,
    tile_ids,
    edge_weight,
    counts,
    boundary,
    cotangent,
):
    nb = features.shape[2] // TILE
    per_pair = boundary.shape[2]
    nx = NX
    nz = nf // (2 * nx)
    chips = nf // 2
    half = chips * ROWS
    chunk = nf * ROWS // ny
    far = ny * ROWS
    lanes = NBANK * nb
    width = ROWS // GROUPS * TILE
    ring_rows = (nz - ZX) * nx * ROWS
    right = ny // 2
    left = ny - 1 - right
    scale = 1.0 / math.sqrt(ny * features.shape[2])
    hbm = pl.BlockSpec(memory_space=pl.ANY)
    dma = pltpu.SemaphoreType.DMA
    act, feature_grad, weight_grad = pl.pallas_call(
        functools.partial(kernel, nf, ny, per_pair, scale),
        out_shape=(
            jax.ShapeDtypeStruct((chips, 2, ROWS, TILE), BF16),
            jax.ShapeDtypeStruct((ROWS, nb * TILE), BF16),
            jax.ShapeDtypeStruct((ROWS, nf * ROWS), F32),
        ),
        in_specs=[hbm] * 9,
        out_specs=(hbm, hbm, hbm),
        scratch_shapes=[
            pltpu.VMEM((chips, 2, ROWS, TILE), BF16),
            pltpu.VMEM((ROWS, nb * TILE), BF16),
            pltpu.VMEM((ROWS, nf * ROWS), F32),
            pltpu.VMEM((per_pair, ny), jnp.int32),
            pltpu.VMEM((ROWS, nb * TILE), BF16),
            pltpu.VMEM((NBANK, TILE, TILE), BF16),
            pltpu.VMEM((K, nb), jnp.int32),
            pltpu.VMEM((K, nb), jnp.int32),
            pltpu.VMEM((K, nb), BF16),
            pltpu.VMEM((1, nb), jnp.int32),
            pltpu.VMEM((chips, 2, ROWS, TILE), BF16),
            pltpu.VMEM((nb * ROWS, TILE), F32),
            pltpu.VMEM((GROUPS, nb, width), BF16),
            pltpu.VMEM((ny, ROWS, width), BF16),
            pltpu.VMEM((ny, ROWS, width), BF16),
            pltpu.VMEM((GROUPS, lanes, width), F32),
            pltpu.VMEM((lanes, 2 * nb), BF16),
            pltpu.VMEM((GROUPS, lanes, 2 * far), BF16),
            pltpu.VMEM((2 * nb, lanes), BF16),
            pltpu.VMEM((2 * far, lanes), BF16),
            pltpu.VMEM((GROUPS, nb, far), BF16),
            pltpu.VMEM((TILE, NBANK * TILE), BF16),
            pltpu.VMEM((ROWS * nb, NBANK * TILE), BF16),
            pltpu.VMEM((nb, ROWS, TILE), BF16),
            pltpu.VMEM((nf, ROWS, TILE), BF16),
            pltpu.VMEM((nf, ROWS, TILE), BF16),
            pltpu.VMEM((2, nz, nx, ROWS, nf * ROWS), BF16),
            pltpu.VMEM((2, half, TILE), BF16),
            pltpu.VMEM((TILE, 2 * half), BF16),
            pltpu.VMEM((half, TILE), BF16),
            pltpu.VMEM((nf, ROWS, TILE), BF16),
            pltpu.VMEM((nf, ROWS, TILE), BF16),
            pltpu.VMEM((GROUPS, lanes, width), BF16),
            pltpu.VMEM((GROUPS, nb, width), F32),
            pltpu.VMEM((ny, ROWS, width), BF16),
            pltpu.VMEM((ny, ROWS, width), BF16),
            pltpu.VMEM((ny, nx, ZX, ROWS, chunk), BF16),
            pltpu.VMEM((ny, nx - 1, ZX, ROWS, chunk), BF16),
            pltpu.VMEM((ny, ZX, ROWS, chunk), BF16),
            pltpu.VMEM((nz * ny, ROWS, chunk), BF16),
            pltpu.VMEM((ny, ring_rows, chunk), F32),
            pltpu.VMEM((right, ring_rows, chunk), BF16),
            pltpu.VMEM((right, ring_rows, chunk), BF16),
            pltpu.VMEM((left, ring_rows, chunk), BF16),
            pltpu.VMEM((left, ring_rows, chunk), BF16),
            pltpu.VMEM(((nz - ZX) * nx, ROWS, chunk), BF16),
            pltpu.VMEM((chips, ROWS, chunk), BF16),
            pltpu.VMEM((ROWS, chunk), F32),
            pltpu.VMEM((ny, ROWS, chunk), F32),
            dma((12,)),
            pltpu.SemaphoreType.REGULAR,
            dma((9,)),
            dma((9,)),
            dma((nz,)),
            dma((nz,)),
            dma((nz,)),
            dma((nz,)),
            dma((nz,)),
            dma((nz,)),
            dma((ny,)),
            dma((ny,)),
            dma((2, right)),
            dma((2, right)),
        ],
        compiler_params=pltpu.CompilerParams(
            collective_id=0,
            has_side_effects=True,
            vmem_limit_bytes=60 * 2**20,
        ),
    )(
        boundary[:, 0, :].T,
        features[0],
        weight,
        tile_bank,
        neighbors[0].T,
        tile_ids[0].T,
        edge_weight[0].T,
        counts,
        cotangent[0].reshape(chips, 2, ROWS, TILE),
    )
    results = (act, feature_grad, weight_grad)
    act, feature_grad, weight_grad = pl.pallas_call(
        hand_over,
        out_shape=tuple(jax.ShapeDtypeStruct(a.shape, a.dtype) for a in results),
        in_specs=[hbm] * 3,
        out_specs=(hbm, hbm, hbm),
        scratch_shapes=[pltpu.VMEM(a.shape, a.dtype) for a in results]
        + [dma((2, 3))],
        compiler_params=pltpu.CompilerParams(vmem_limit_bytes=60 * 2**20),
    )(*results)
    return (
        act.reshape(cotangent.shape),
        feature_grad[None],
        weight_grad,
    )


def solution(mesh):
    in_specs = (
        P("dom", "feat", None),
        P("feat", None),
        P(),
        P("dom", None, None),
        P("dom", None, None),
        P("dom", None, None),
        P("dom", None),
        P(None, "dom", None),
        P("dom", None, "feat"),
    )
    out_specs = (P("dom", None, "feat"), P("dom", "feat", None), P("feat", None))
    return jax.shard_map(
        functools.partial(per_device, mesh.shape["feat"], mesh.shape["dom"]),
        mesh=mesh,
        in_specs=in_specs,
        out_specs=out_specs,
        check_vma=False,
    )
```
